128 devices in a mesh: dp: 8 (over y, core), ctx: 16 (over z, x).
Axes of the slice: x: 4, y: 4, z: 4, core: 2. Of those that a mesh axis runs over, the one named last changes fastest.
Arguments:
- queries: bfloat16 [8, 3072, 4096], P('dp', 'ctx'), may hold values from -32 to 32
- keys: bfloat16 [8, 3072, 1024], P('dp', 'ctx'), may hold values from -6 to 6
- values: bfloat16 [8, 3072, 1024], P('dp', 'ctx'), may hold values from -6 to 6
- segment_ids: int32 [8, 3072], P('dp', 'ctx'), may hold values from 0 to 5, never falling along the last dimension, each value on 1 to 1536 neighbouring positions
- ssd_input: float32 [8, 3072, 4096], P('dp', 'ctx'), may hold values from -6 to 6
- b_matrix: float32 [8, 3072, 1024], P('dp', 'ctx'), may hold values from -0.5 to 0.5
- c_matrix: float32 [8, 3072, 1024], P('dp', 'ctx'), may hold values from -0.5 to 0.5
- step_size: float32 [8, 64, 3072], P('dp', None, 'ctx'), may hold values from 0.5 to 5376
- decay_log: float32 [64], replicated
- skip_gain: float32 [64], replicated, may hold values from 0.1 to 1.9
- cotangent: float32 [8, 3072, 4096], P('dp', 'ctx'), may hold values from -6 to 6
Outputs:
- attention_out: bfloat16 [8, 3072, 4096], P('dp', 'ctx')
- mixer_out: bfloat16 [8, 3072, 4096], P('dp', 'ctx')
- decay_grad: float32 [64], replicated
The draws below stay inside these ranges and needn't reach their ends.
All inputs are finite; a program needn't handle non-finite values.
Results may differ from the reference program's by a relative error of at most 0.009.
Values may be sent and summed in bfloat16 or wider, within the bound.
A program may use at most 256 MiB of HBM per device.

```python
import math
import jax
import jax.numpy as jnp
import numpy as np
from jax import lax

Q_HEADS = 32
KV_HEADS = 8
HEAD_WIDTH = 128
SSD_HEADS = 64
HEAD_P = 64
STATE = 128
GROUPS = 8
TOK_DEV = 192
SEGS = 6
TRACE_SPAN_SIZE = 3072
MAXTRAJ = 1536
N_DP = 8


def attention_base(key):
    shape = (N_DP, TRACE_SPAN_SIZE, KV_HEADS * HEAD_WIDTH)
    starting_position = jnp.clip(jax.random.normal(jax.random.fold_in(key, 1), shape, jnp.float32), -6.0, 6.0)
    return starting_position


def draw_keys(key, part):
    starting_position = attention_base(key)
    return starting_position.astype(jnp.bfloat16)


def draw_queries(key, part):
    key = jax.random.fold_in(key, 12)
    fresh = jnp.clip(jax.random.normal(key, (N_DP, TRACE_SPAN_SIZE, Q_HEADS * HEAD_WIDTH), jnp.float32), -6.0, 6.0)
    return fresh.astype(jnp.bfloat16)


def decay_rates(key, slow_share):
    pick = jax.random.uniform(jax.random.fold_in(key, 21), (SSD_HEADS,))
    spread = jax.random.uniform(jax.random.fold_in(key, 22), (SSD_HEADS,))
    slow = jnp.log(0.2 / MAXTRAJ) + spread * jnp.log(5.0)
    fast = jnp.log(1.0 / 50.0) + spread * jnp.log(50.0 / 30.0)
    return jnp.where(pick < slow_share, slow, fast)


def draw_decay_log(key, part):
    share = 0.5
    forgetting_speeds = decay_rates(key, share)
    return forgetting_speeds


def draw_step_size(key, part):
    share = 0.5
    forgetting_speeds = decay_rates(key, share)
    key = jax.random.fold_in(key, 31)
    starting_position = jnp.exp(jax.random.uniform(jax.random.fold_in(key, 1), (N_DP, SSD_HEADS, TRACE_SPAN_SIZE), jnp.float32, jnp.log(0.5), jnp.log(2.0)))
    segment_stretch = jax.random.uniform(jax.random.fold_in(key, 2), (N_DP, 1, TRACE_SPAN_SIZE)) < 4.0 / TRACE_SPAN_SIZE
    dropped_quantity = jax.random.uniform(jax.random.fold_in(key, 3), (N_DP, 1, TRACE_SPAN_SIZE), jnp.float32, 0.22, 0.7)
    return jnp.where(segment_stretch, dropped_quantity / jnp.exp(forgetting_speeds)[None, :, None], starting_position)


def block_scale(stream_key, shape, split, smallest, largest):
    level, own = 1.0, jax.random.fold_in(stream_key, 6)
    for dim, shards_of in split:
        draws = jnp.exp(jax.random.uniform(jax.random.fold_in(own, dim), (shards_of,), jnp.float32, smallest / len(split), largest / len(split)))
        level = level * jnp.repeat(draws, shape[dim] // shards_of).reshape([-1 if axis == dim else 1 for axis in range(len(shape))])
    return level


def split_up(count, total, limit, lean):
    portions = [(1 << 20) // math.isqrt(grade ** lean) + 1 for grade in range(2, count + 1)]
    rest, counts = total - limit - (count - 1), [1] * (count - 1)
    while rest > 0:
        movable = [i for i in range(count - 1) if counts[i] < limit]
        whole, left = sum([portions[i] for i in movable]), rest
        for i in movable:
            addition = min(limit - counts[i], max(1, left * portions[i] // whole), rest)
            counts[i] = counts[i] + addition
            rest = rest - addition
    return np.array([limit] + counts)


def uneven_parts(own_key, number_of, total, reach, slope):
    if number_of == 2:
        one = jax.random.randint(own_key, (), max(1, total - reach), min(reach, total - 1) + 1)
        return jnp.stack([one, total - one])
    sizes = jnp.asarray(split_up(number_of, total, reach, slope), jnp.int32)
    couples = (number_of - 1) // 2
    donor, receiver = sizes[1:1 + 2 * couples:2], sizes[2:2 + 2 * couples:2]
    margin = jnp.minimum(donor - 1, reach - receiver)
    shifted = jax.random.randint(jax.random.fold_in(own_key, 1), (couples,), 0, 1 << 20) % (margin + 1)
    sizes = sizes.at[1:1 + 2 * couples:2].set(donor - shifted).at[2:2 + 2 * couples:2].set(receiver + shifted)
    return sizes[jax.random.permutation(jax.random.fold_in(own_key, 2), number_of)]


def centred(key, dims, scale, limit, shards=(), held_as=jnp.bfloat16):
    values = jax.random.normal(key, dims, jnp.float32) * scale
    if len(shards) > 0:
        values = block_scale(key, dims, shards, -0.22, 0.18) * values
    return jnp.clip(values, min=-limit, max=limit).astype(held_as)


def setup_inputs(seed: int = 0) -> dict:
    key_of = jax.random.split(jax.random.key(seed), 12)
    return {
        "queries": draw_queries(jax.random.fold_in(key_of[11], 71), 0),
        "keys": draw_keys(jax.random.fold_in(key_of[11], 71), 0),
        "values": centred(key_of[2], (N_DP, TRACE_SPAN_SIZE, KV_HEADS * HEAD_WIDTH), 1.0, 6.0, ((0, 8), (1, 16))),
        "segment_ids": jax.vmap(lambda own: jnp.searchsorted(jnp.cumsum(uneven_parts(own, SEGS, TRACE_SPAN_SIZE, MAXTRAJ, 0)), jnp.arange(TRACE_SPAN_SIZE), side="right"))(jax.random.split(key_of[3], N_DP)).reshape((N_DP, TRACE_SPAN_SIZE)).astype(jnp.int32),
        "ssd_input": centred(key_of[4], (N_DP, TRACE_SPAN_SIZE, SSD_HEADS * HEAD_P), 1.0, 6.0, ((0, 8), (1, 16)), jnp.float32),
        "b_matrix": centred(key_of[5], (N_DP, TRACE_SPAN_SIZE, GROUPS * STATE), STATE ** -0.5, 0.5, ((0, 8), (1, 16)), jnp.float32),
        "c_matrix": centred(key_of[6], (N_DP, TRACE_SPAN_SIZE, GROUPS * STATE), STATE ** -0.5, 0.5, ((0, 8), (1, 16)), jnp.float32),
        "step_size": draw_step_size(jax.random.fold_in(key_of[11], 71), 0),
        "decay_log": draw_decay_log(jax.random.fold_in(key_of[11], 71), 0),
        "skip_gain": jnp.clip(1.0 + 0.18 * jax.random.normal(key_of[9], (SSD_HEADS,), jnp.float32), 0.1, 1.9),
        "cotangent": centred(key_of[10], (N_DP, TRACE_SPAN_SIZE, SSD_HEADS * HEAD_P), 1.0, 6.0, ((0, 8), (1, 16)), jnp.float32),
    }


precise = lax.Precision.HIGHEST


def join_states(earlier, later):
    span_a, state_a, hat_a, last_a = earlier
    span_b, state_b, hat_b, last_b = later
    linked = jnp.logical_or(last_a == last_b, last_b < 0.0)
    multiplier = jnp.where(linked, jnp.exp(span_b), 0.0)[..., None, None]
    state = multiplier * state_a + state_b
    hat = multiplier * (hat_a + span_b[..., None, None] * state_a) + hat_b
    last = jnp.where(last_b < 0.0, last_a, last_b)
    return (span_a + span_b, state, hat, last)


def decay_parts(step_blk, decay_log, groups):
    heads, count = step_blk.shape
    logs = step_blk * (-jnp.exp(decay_log))[:, None]
    return jnp.cumsum(logs, axis=1).reshape(groups, heads // groups, count)


def local_part(input_blk, b_blk, c_blk, forgetting_accrued, segment, grad_blk):
    count = input_blk.shape[0]
    groups, per_group = forgetting_accrued.shape[0], forgetting_accrued.shape[1]
    inputs4 = input_blk.reshape(count, groups, per_group, -1)
    grads4 = grad_blk.reshape(count, groups, per_group, -1)
    b_groups = b_blk.reshape(count, groups, -1)
    c_groups = c_blk.reshape(count, groups, -1)
    place = jnp.arange(count, dtype=jnp.int32)
    mask = (place[None, :] <= place[:, None]) & (segment[None, :] == segment[:, None])
    gap = jnp.where(mask, forgetting_accrued[:, :, :, None] - forgetting_accrued[:, :, None, :], 0.0)
    inner = jnp.einsum("tgn,sgn->gts", c_groups, b_groups, precision=precise)
    weight = jnp.where(mask, jnp.exp(gap), 0.0) * inner[:, None]
    near = jnp.einsum("ghts,sghp->tghp", weight, inputs4, precision=precise)
    pairs = jnp.einsum("tghp,sghp->ghts", grads4, inputs4, precision=precise)
    grad_near = jnp.sum(weight * gap * pairs, axis=(2, 3)).reshape(-1)
    tail = forgetting_accrued[:, :, -1:] - forgetting_accrued
    keep = segment == segment[-1]
    end_weight = jnp.where(keep[None, None, :], jnp.exp(tail), 0.0)
    state_own = jnp.einsum("sgn,ghs,sghp->ghnp", b_groups, end_weight, inputs4, precision=precise)
    hat_own = jnp.einsum("sgn,ghs,sghp->ghnp", b_groups, end_weight * tail, inputs4, precision=precise)
    element = (forgetting_accrued[:, :, -1], state_own, hat_own, segment[-1].astype(jnp.float32))
    return near.reshape(count, -1), grad_near, element


def carried_part(c_blk, forgetting_accrued, segment, grad_blk, state_in, hat_in, last_in):
    count = c_blk.shape[0]
    groups, per_group = forgetting_accrued.shape[0], forgetting_accrued.shape[1]
    c_groups = c_blk.reshape(count, groups, -1)
    grads4 = grad_blk.reshape(count, groups, per_group, -1)
    live = segment.astype(jnp.float32) == last_in
    scale = jnp.where(live[None, None, :], jnp.exp(forgetting_accrued), 0.0).transpose(2, 0, 1)[..., None]
    sum_t = forgetting_accrued.transpose(2, 0, 1)[..., None]
    starting_position = jnp.einsum("tgn,ghnp->tghp", c_groups, state_in, precision=precise)
    extra = jnp.einsum("tgn,ghnp->tghp", c_groups, hat_in, precision=precise)
    far = starting_position * scale
    grad_far = jnp.sum(grads4 * (extra + sum_t * starting_position) * scale, axis=(0, 3)).reshape(-1)
    return far.reshape(count, -1), grad_far


def mixer_row(input_row, b_row, c_row, step_row, segment_row, grad_row, decay_log, skip_gain):
    per_group = SSD_HEADS // GROUPS
    skip_full = jnp.repeat(skip_gain, HEAD_P)

    def advance(carry, turn):
        first = turn * TOK_DEV
        input_blk = lax.dynamic_slice_in_dim(input_row, first, TOK_DEV, 0)
        b_blk = lax.dynamic_slice_in_dim(b_row, first, TOK_DEV, 0)
        c_blk = lax.dynamic_slice_in_dim(c_row, first, TOK_DEV, 0)
        grad_blk = lax.dynamic_slice_in_dim(grad_row, first, TOK_DEV, 0)
        segment = lax.dynamic_slice_in_dim(segment_row, first, TOK_DEV, 0)
        step_blk = lax.dynamic_slice_in_dim(step_row, first, TOK_DEV, 1)
        forgetting_accrued = decay_parts(step_blk, decay_log, GROUPS)
        near, grad_near, element = local_part(input_blk, b_blk, c_blk, forgetting_accrued, segment, grad_blk)
        far, grad_far = carried_part(c_blk, forgetting_accrued, segment, grad_blk, carry[1], carry[2], carry[3])
        mixed = near + far + input_blk * skip_full[None, :]
        return join_states(carry, element), (mixed, grad_near + grad_far)

    start = (jnp.zeros((GROUPS, per_group), jnp.float32),
             jnp.zeros((GROUPS, per_group, STATE, HEAD_P), jnp.float32),
             jnp.zeros((GROUPS, per_group, STATE, HEAD_P), jnp.float32),
             jnp.array(-1.0, jnp.float32))
    final, (mixed, grads) = lax.scan(advance, start, jnp.arange(TRACE_SPAN_SIZE // TOK_DEV, dtype=jnp.int32))
    return mixed.reshape(TRACE_SPAN_SIZE, -1), jnp.sum(grads, axis=0)


def attend_row(query_row, key_row, value_row, segment_row):
    block = min(512, TRACE_SPAN_SIZE)
    span = min(MAXTRAJ + block, TRACE_SPAN_SIZE)
    repeat_count = Q_HEADS // KV_HEADS

    def one_block(turn):
        first = turn * block
        key_first = jnp.maximum(first + block - span, 0).astype(jnp.int32)
        query_block = lax.dynamic_slice_in_dim(query_row, first, block, 0).reshape(block, KV_HEADS, repeat_count, HEAD_WIDTH)
        key_block = lax.dynamic_slice_in_dim(key_row, key_first, span, 0).reshape(span, KV_HEADS, HEAD_WIDTH)
        value_block = lax.dynamic_slice_in_dim(value_row, key_first, span, 0).reshape(span, KV_HEADS, HEAD_WIDTH)
        segment_q = lax.dynamic_slice_in_dim(segment_row, first, block, 0)
        segment_k = lax.dynamic_slice_in_dim(segment_row, key_first, span, 0)
        query_pos = first + jnp.arange(block, dtype=jnp.int32)
        key_pos = key_first + jnp.arange(span, dtype=jnp.int32)
        mask = (key_pos[None, :] <= query_pos[:, None]) & (segment_k[None, :] == segment_q[:, None])
        score_matrix = jnp.einsum("fkhu,nku->khfn", query_block.astype(jnp.float32), key_block.astype(jnp.float32)) * (HEAD_WIDTH ** -0.5)
        row_top = jnp.max(jnp.where(mask, score_matrix, -1e30), axis=-1)
        exponent_weight = jnp.where(mask, jnp.exp(score_matrix - row_top[..., None]), 0.0)
        total = jnp.sum(exponent_weight, axis=-1)
        rounded_value = lax.optimization_barrier(exponent_weight.astype(jnp.bfloat16)).astype(jnp.float32)
        summed_total = jnp.einsum("kvuc,ckw->ukvw", rounded_value, value_block.astype(jnp.float32))
        result = summed_total / total.transpose(2, 0, 1)[..., None]
        return result.reshape(block, -1).astype(jnp.bfloat16)

    blocks = lax.map(one_block, jnp.arange(TRACE_SPAN_SIZE // block, dtype=jnp.int32))
    return blocks.reshape(TRACE_SPAN_SIZE, -1)


def reference(queries, keys, values, segment_ids, ssd_input, b_matrix, c_matrix, step_size, decay_log, skip_gain, cotangent):
    attention_out = lax.map(lambda items: attend_row(*items), (queries, keys, values, segment_ids))

    def mixer_one(items):
        return mixer_row(items[0], items[1], items[2], items[3], items[4], items[5], decay_log, skip_gain)

    mixed, grads = lax.map(mixer_one, (ssd_input, b_matrix, c_matrix, step_size, segment_ids, cotangent))
    decay_grad = jnp.sum(grads, axis=0) / (N_DP * TRACE_SPAN_SIZE)
    return attention_out, mixed.astype(jnp.bfloat16), decay_grad
```

```python
import functools
import math

import jax
import jax.numpy as jnp
from jax import lax
from jax.experimental import pallas as pl
from jax.experimental.pallas import tpu as pltpu
from jax.sharding import PartitionSpec as P

Q_HEADS = 32
KV_HEADS = 8
REP = Q_HEADS // KV_HEADS
WIDTH = 128
SSD_HEADS = 64
HEAD_P = 64
STATE = 128
GROUPS = 8
PER = SSD_HEADS // GROUPS
GW = PER * HEAD_P
COLS = 4
ROWS = 4
KVW = 2 * KV_HEADS * WIDTH + WIDTH
FAR_BELOW = -1e30
MESH = pl.DeviceIdType.MESH

OWN, P1, P2, AB1, AB3, AB2, BC1, BC3, BC2 = range(9)
BACK = (0, 4, 8, 1, 3, 2, 5, 7, 6)

f32, bf16 = jnp.float32, jnp.bfloat16


def dot(a, b, ca, cb, precision=None):
    return lax.dot_general(
        a, b, (((ca,), (cb,)), ((), ())), precision=precision, preferred_element_type=f32
    )


def kernel(
    q_ref, k_ref, v_ref, seg_ref, x_ref, b_ref, c_ref, logs_ref, skip_ref, g_ref,
    ao_ref, mo_ref, dgn_ref, dgf_ref,
    kvb, qs, acc, mrow, lrow, bias, st_own, st_row, meta_own, meta_row,
    r_out, r_meta, r_in, r_meta_in, f_out, f_in, d_ref, dh_ref, fexp_ref, near_ref,
    kv_ss, kv_rs, a_ss, a_rs, am_ss, am_rs, r_ss, r_rs, rm_ss, rm_rs, f_ss, f_rs,
):
    count = q_ref.shape[0]
    me = lax.axis_index("ctx")
    z, x = me // COLS, me % COLS

    def dev(dz, dx):
        return {"ctx": ((z + dz) % ROWS) * COLS + (x + dx) % COLS}

    barrier = pltpu.get_barrier_semaphore()
    partners = [(0, 1), (0, 2), (0, 3), (1, 0), (2, 0), (3, 0)]
    for dz, dx in partners:
        pl.semaphore_signal(barrier, inc=1, device_id=dev(dz, dx), device_id_type=MESH)

    segrow = seg_ref[...].astype(f32)
    rr = lax.broadcasted_iota(jnp.int32, (count, count), 0)
    cc = lax.broadcasted_iota(jnp.int32, (count, count), 1)
    eye = rr == cc
    segcol = jnp.sum(jnp.where(eye, segrow, 0.0), axis=1, keepdims=True)
    lane = lax.broadcasted_iota(jnp.int32, (count, WIDTH), 1).astype(f32)
    onehot = jnp.where(lane == segcol, 1.0, 0.0).astype(bf16)
    other = jnp.where((lane != segcol) & (lane < 8.0), FAR_BELOW, 0.0).astype(bf16)
    kvb[OWN, :, : KV_HEADS * WIDTH] = k_ref[...]
    kvb[OWN, :, KV_HEADS * WIDTH : 2 * KV_HEADS * WIDTH] = v_ref[...]
    kvb[OWN, :, 2 * KV_HEADS * WIDTH :] = other

    pl.semaphore_wait(barrier, len(partners))

    def kv_copy(src, slot, dz, dx):
        return pltpu.make_async_remote_copy(
            src_ref=kvb.at[src], dst_ref=kvb.at[slot], send_sem=kv_ss.at[slot],
            recv_sem=kv_rs.at[slot], device_id=dev(dz, dx), device_id_type=MESH,
        )

    @pl.when(z < 3)
    def _():
        kv_copy(OWN, P1, 1, 0).start()

    for slot, d in ((AB1, 1), (AB3, 3), (AB2, 2)):
        @pl.when(x + d < COLS)
        def _(slot=slot, d=d):
            kv_copy(OWN, slot, 0, d).start()

    @pl.when(z < 2)
    def _():
        kv_copy(OWN, P2, 2, 0).start()

    mask = (cc <= rr) & (segrow == segcol)
    upper = jnp.where(rr <= cc, 1.0, 0.0)
    eyef = jnp.where(eye, 1.0, 0.0)
    keep = jnp.where(segrow == segrow[:, count - 1 : count], 1.0, 0.0)
    live = jnp.where(segrow == segrow[:, 0:1], 1.0, 0.0)
    h16 = lax.broadcasted_iota(jnp.int32, (2 * PER, GW), 0) % PER
    spread = jnp.where(h16 == lax.broadcasted_iota(jnp.int32, (2 * PER, GW), 1) // HEAD_P, 1.0, 0.0)
    spread_bf = spread.astype(bf16)
    hi = lax.Precision.HIGHEST
    low_half = lax.broadcasted_iota(jnp.int32, (count, 2 * HEAD_P), 1) < HEAD_P
    meta_rows = lax.broadcasted_iota(jnp.int32, (8, GW), 0)
    last_own, first_own = segrow[:, count - 1 : count], segrow[:, 0:1]

    def expand(value):
        top = value.astype(bf16)
        rest = (value - top.astype(f32)).astype(bf16)
        return dot(jnp.concatenate([top, rest], axis=0), spread_bf, 0, 0)

    def mixer_group(g, _):
        cols = pl.ds(pl.multiple_of(g * GW, GW), GW)
        ncols = pl.ds(pl.multiple_of(g * STATE, STATE), STATE)
        cs = dot(logs_ref[pl.ds(pl.multiple_of(g * PER, PER), PER), :], upper, 1, 0, hi)
        cst = dot(eyef, cs, 1, 1, hi)
        span = cs[:, count - 1 : count]
        tail = span - cs
        e = jnp.exp(tail) * keep
        f = jnp.exp(cs) * live
        xg, gg = x_ref[:, cols], g_ref[:, cols]
        bg, cg = b_ref[:, ncols].astype(bf16), c_ref[:, ncols].astype(bf16)
        right = jnp.concatenate([(xg * expand(e)).astype(bf16), (xg * expand(e * tail)).astype(bf16)], axis=1)
        sh = dot(bg, right, 0, 0).astype(bf16)
        st_own[g // 2, g % 2] = sh[:, :GW]
        st_own[g // 2, 2 + g % 2] = sh[:, GW:]
        fe = expand(f)
        fexp_ref[g] = fe
        right = jnp.concatenate([(gg * fe).astype(bf16), (gg * expand(f * cs)).astype(bf16)], axis=1)
        dd = dot(cg, right, 0, 0)
        d_ref[g] = dd[:, :GW]
        dh_ref[g] = dd[:, GW:]
        span_row = jnp.sum(spread[:PER] * span, axis=0, keepdims=True)
        meta = jnp.where(meta_rows == 0, span_row, jnp.where(meta_rows == 1, last_own, first_own))
        meta_own[g // 2, :, pl.ds(pl.multiple_of((g % 2) * GW, GW), GW)] = meta
        inner = dot(cg, bg, 1, 1)
        sums = []
        for pair in range(PER // 2):
            lanes = slice(pair * 2 * HEAD_P, (pair + 1) * 2 * HEAD_P)
            xp, gp = xg[:, lanes], gg[:, lanes]
            xpb, gpb = xp.astype(bf16), gp.astype(bf16)
            near = None
            for half in range(2):
                j = pair * 2 + half
                mine = low_half if half == 0 else jnp.logical_not(low_half)
                gap = jnp.where(mask, cst[:, j : j + 1] - cs[j : j + 1, :], FAR_BELOW)
                weight = jnp.exp(gap) * inner
                pairs = dot(jnp.where(mine, gpb, jnp.zeros_like(gpb)), xpb, 1, 1)
                sums.append(jnp.sum(weight * gap * pairs, axis=0, keepdims=True))
                part = dot(weight.astype(bf16), jnp.where(mine, xpb, jnp.zeros_like(xpb)), 1, 0)
                near = part if near is None else near + part
            at = pl.ds(pl.multiple_of(g * GW + pair * 2 * HEAD_P, 2 * HEAD_P), 2 * HEAD_P)
            near_ref[:, at] = near + xp * skip_ref[:, at]
        dgn_ref[pl.ds(pl.multiple_of(g * PER, PER), PER), :] = jnp.concatenate(sums, axis=0)
        return 0

    lax.fori_loop(0, GROUPS, mixer_group, 0)

    def a_copy(d):
        to = (x + d) % COLS
        return pltpu.make_async_remote_copy(
            src_ref=st_own.at[to], dst_ref=st_row.at[x], send_sem=a_ss.at[d - 1],
            recv_sem=a_rs.at[d - 1], device_id=dev(0, d), device_id_type=MESH,
        )

    def am_copy(d):
        to = (x + d) % COLS
        return pltpu.make_async_remote_copy(
            src_ref=meta_own.at[to], dst_ref=meta_row.at[x], send_sem=am_ss.at[d - 1],
            recv_sem=am_rs.at[d - 1], device_id=dev(0, d), device_id_type=MESH,
        )

    for d in (1, 3, 2):
        am_copy(d).start()
        a_copy(d).start()
    st_row[x] = st_own[x]
    meta_row[x] = meta_own[x]

    for h in range(KV_HEADS):
        for r in range(REP):
            head = h * REP + r
            qs[h, r * count : (r + 1) * count, :WIDTH] = q_ref[:, head * WIDTH : (head + 1) * WIDTH]
            qs[h, r * count : (r + 1) * count, WIDTH:] = onehot
    causal = jnp.where(rr <= cc, 0.0, FAR_BELOW)
    bias[...] = jnp.concatenate([causal] * REP, axis=1)
    scale = math.log2(math.e) / math.sqrt(WIDTH)

    def scores(slot, h):
        at = pl.ds(pl.multiple_of(h * WIDTH, WIDTH), WIDTH)
        kk = jnp.concatenate([kvb[slot, :, at], kvb[slot, :, 2 * KV_HEADS * WIDTH :]], axis=1)
        return dot(kk, qs[h], 1, 1)

    def values_of(slot, h):
        return kvb[slot, :, pl.ds(pl.multiple_of((KV_HEADS + h) * WIDTH, WIDTH), WIDTH)]

    def own_head(h, _):
        s = scores(OWN, h) + bias[...]
        top = jnp.max(s, axis=0, keepdims=True)
        w = jnp.exp2((s - top) * scale)
        mrow[pl.ds(h, 1), :] = top
        lrow[pl.ds(h, 1), :] = jnp.sum(w, axis=0, keepdims=True)
        acc[h] = dot(values_of(OWN, h), w.astype(bf16), 0, 0)
        return 0

    lax.fori_loop(0, KV_HEADS, own_head, 0)

    def attend(slot):
        def head(h, _):
            s = scores(slot, h)
            before = mrow[pl.ds(h, 1), :]
            top = jnp.maximum(before, jnp.max(s, axis=0, keepdims=True))
            w = jnp.exp2((s - top) * scale)
            fade = jnp.exp2((before - top) * scale)
            mrow[pl.ds(h, 1), :] = top
            lrow[pl.ds(h, 1), :] = lrow[pl.ds(h, 1), :] * fade + jnp.sum(w, axis=0, keepdims=True)
            acc[h] = acc[h] * fade + dot(values_of(slot, h), w.astype(bf16), 0, 0)
            return 0

        lax.fori_loop(0, KV_HEADS, head, 0)

    def arrive(slot):
        kv_copy(OWN, slot, 0, 1).wait_recv()

    @pl.when(z >= 1)
    def _():
        arrive(P1)
        for slot, d in ((AB1, 1), (AB3, 3), (AB2, 2)):
            @pl.when(x + d >= COLS)
            def _(slot=slot, d=d):
                kv_copy(P1, slot, 0, d).start()
        for slot, d in ((BC1, 1), (BC3, 3)):
            @pl.when(x + d < COLS)
            def _(slot=slot, d=d):
                kv_copy(P1, slot, 0, d).start()

    for d in (1, 3, 2):
        am_copy(d).wait_recv()
        a_copy(d).wait_recv()

    def row_meta(k, c, at):
        return meta_row[k, at : at + 1, c * GW : (c + 1) * GW]

    for c in range(2):
        s, hat = st_row[0, c].astype(f32), st_row[0, 2 + c].astype(f32)
        total, last = row_meta(0, c, 0), row_meta(0, c, 1)
        for k in range(1, COLS):
            span, after = row_meta(k, c, 0), row_meta(k, c, 1)
            fade = jnp.where(last == after, jnp.exp(span), 0.0)
            hat = fade * (hat + span * s) + st_row[k, 2 + c].astype(f32)
            s = fade * s + st_row[k, c].astype(f32)
            total, last = total + span, after
        r_out[c] = s.astype(bf16)
        r_out[2 + c] = hat.astype(bf16)
        r_meta[:, c * GW : (c + 1) * GW] = jnp.where(meta_rows == 0, total, last)

    def r_copy(dz):
        return pltpu.make_async_remote_copy(
            src_ref=r_out, dst_ref=r_in.at[dz - 1], send_sem=r_ss.at[dz - 1],
            recv_sem=r_rs.at[dz - 1], device_id=dev(dz, 0), device_id_type=MESH,
        )

    def rm_copy(dz):
        return pltpu.make_async_remote_copy(
            src_ref=r_meta, dst_ref=r_meta_in.at[dz - 1], send_sem=rm_ss.at[dz - 1],
            recv_sem=rm_rs.at[dz - 1], device_id=dev(dz, 0), device_id_type=MESH,
        )

    for dz in (1, 2):
        @pl.when(z + dz < ROWS)
        def _(dz=dz):
            rm_copy(dz).start()
            r_copy(dz).start()

        @pl.when(z - dz < 0)
        def _(dz=dz):
            r_in[dz - 1] = jnp.zeros_like(r_in[dz - 1])
            r_meta_in[dz - 1] = jnp.full_like(r_meta_in[dz - 1], -1.0)

    for slot in (AB1, AB3):
        @pl.when(me >= BACK[slot])
        def _(slot=slot):
            arrive(slot)
            attend(slot)

    @pl.when(z >= 2)
    def _():
        arrive(P2)
        for slot, d in ((BC1, 1), (BC3, 3)):
            @pl.when(x + d >= COLS)
            def _(slot=slot, d=d):
                kv_copy(P2, slot, 0, d).start()

    @pl.when(me >= BACK[AB2])
    def _():
        arrive(AB2)

        @pl.when(z < 3)
        def _():
            kv_copy(AB2, BC2, 1, 0).start()

        attend(AB2)

    for dz in (1, 2):
        @pl.when(z - dz >= 0)
        def _(dz=dz):
            rm_copy(dz).wait_recv()
            r_copy(dz).wait_recv()

    for c in range(2):
        lanes = slice(c * GW, (c + 1) * GW)
        span, last = r_meta_in[0, 0:1, lanes], r_meta_in[0, 1:2, lanes]
        fade = jnp.where(r_meta_in[1, 1:2, lanes] == last, jnp.exp(span), 0.0)
        s2, hat2 = r_in[1, c].astype(f32), r_in[1, 2 + c].astype(f32)
        hat = fade * (hat2 + span * s2) + r_in[0, 2 + c].astype(f32)
        s = fade * s2 + r_in[0, c].astype(f32)
        for k in range(COLS):
            goes_on = jnp.where(row_meta(k, c, 2) == last, 1.0, 0.0)
            f_out[k, c] = (s * goes_on).astype(bf16)
            f_out[k, 2 + c] = (hat * goes_on).astype(bf16)
            if k < COLS - 1:
                span, after = row_meta(k, c, 0), row_meta(k, c, 1)
                fade = jnp.where(last == after, jnp.exp(span), 0.0)
                hat = fade * (hat + span * s) + st_row[k, 2 + c].astype(f32)
                s = fade * s + st_row[k, c].astype(f32)
                last = after

    def f_copy(d):
        to = (x + d) % COLS
        return pltpu.make_async_remote_copy(
            src_ref=f_out.at[to], dst_ref=f_in.at[x], send_sem=f_ss.at[d - 1],
            recv_sem=f_rs.at[d - 1], device_id=dev(0, d), device_id_type=MESH,
        )

    for d in (1, 3, 2):
        f_copy(d).start()
    f_in[x] = f_out[x]

    @pl.when(me >= BACK[P1])
    def _():
        attend(P1)

    @pl.when(me >= BACK[P2])
    def _():
        attend(P2)

    for slot in (BC1, BC3, BC2):
        @pl.when(me >= BACK[slot])
        def _(slot=slot):
            arrive(slot)
            attend(slot)

    for d in (1, 3, 2):
        f_copy(d).wait_recv()

    def far_group(g, _):
        cols = pl.ds(pl.multiple_of(g * GW, GW), GW)
        ncols = pl.ds(pl.multiple_of(g * STATE, STATE), STATE)
        s_in, hat_in = f_in[g // 2, g % 2], f_in[g // 2, 2 + g % 2]
        far = dot(c_ref[:, ncols].astype(bf16), s_in, 1, 0) * fexp_ref[g]
        mo_ref[:, cols] = (near_ref[:, cols] + far).astype(bf16)
        terms = hat_in.astype(f32) * d_ref[g] + s_in.astype(f32) * dh_ref[g]
        dgf_ref[pl.ds(g, 1), :] = jnp.sum(terms, axis=0, keepdims=True)
        return 0

    lax.fori_loop(0, GROUPS, far_group, 0)

    for h in range(KV_HEADS):
        out = (acc[h] / lrow[h : h + 1, :]).T.astype(bf16)
        for r in range(REP):
            head = h * REP + r
            ao_ref[:, head * WIDTH : (head + 1) * WIDTH] = out[r * count : (r + 1) * count]

    @pl.when(z < 3)
    def _():
        kv_copy(OWN, P1, 1, 0).wait_send()

    @pl.when(z < 2)
    def _():
        kv_copy(OWN, P2, 2, 0).wait_send()

    for slot, d in ((AB1, 1), (AB3, 3), (AB2, 2)):
        @pl.when((x + d < COLS) | (z >= 1))
        def _(slot=slot, d=d):
            kv_copy(OWN, slot, 0, d).wait_send()

    for slot, d in ((BC1, 1), (BC3, 3)):
        @pl.when(z >= 1 + (x + d) // COLS)
        def _(slot=slot, d=d):
            kv_copy(OWN, slot, 0, d).wait_send()

    @pl.when((me >= BACK[AB2]) & (z < 3))
    def _():
        kv_copy(OWN, BC2, 1, 0).wait_send()

    for d in (1, 3, 2):
        am_copy(d).wait_send()
        a_copy(d).wait_send()
        f_copy(d).wait_send()
    for dz in (1, 2):
        @pl.when(z + dz < ROWS)
        def _(dz=dz):
            rm_copy(dz).wait_send()
            r_copy(dz).wait_send()


def fused(q, k, v, seg, x, b, c, logs, skip, g):
    count = q.shape[0]
    vmem = pl.BlockSpec(memory_space=pltpu.VMEM)
    dma = pltpu.SemaphoreType.DMA
    return pl.pallas_call(
        kernel,
        out_shape=(
            jax.ShapeDtypeStruct((count, Q_HEADS * WIDTH), bf16),
            jax.ShapeDtypeStruct((count, SSD_HEADS * HEAD_P), bf16),
            jax.ShapeDtypeStruct((SSD_HEADS, count), f32),
            jax.ShapeDtypeStruct((GROUPS, GW), f32),
        ),
        in_specs=[vmem] * 10,
        out_specs=(vmem,) * 4,
        scratch_shapes=[
            pltpu.VMEM((9, count, KVW), bf16),
            pltpu.VMEM((KV_HEADS, REP * count, 2 * WIDTH), bf16),
            pltpu.VMEM((KV_HEADS, WIDTH, REP * count), f32),
            pltpu.VMEM((KV_HEADS, REP * count), f32),
            pltpu.VMEM((KV_HEADS, REP * count), f32),
            pltpu.VMEM((count, REP * count), f32),
            pltpu.VMEM((COLS, 4, STATE, GW), bf16),
            pltpu.VMEM((COLS, 4, STATE, GW), bf16),
            pltpu.VMEM((COLS, 8, 2 * GW), f32),
            pltpu.VMEM((COLS, 8, 2 * GW), f32),
            pltpu.VMEM((4, STATE, GW), bf16),
            pltpu.VMEM((8, 2 * GW), f32),
            pltpu.VMEM((2, 4, STATE, GW), bf16),
            pltpu.VMEM((2, 8, 2 * GW), f32),
            pltpu.VMEM((COLS, 4, STATE, GW), bf16),
            pltpu.VMEM((COLS, 4, STATE, GW), bf16),
            pltpu.VMEM((GROUPS, STATE, GW), f32),
            pltpu.VMEM((GROUPS, STATE, GW), f32),
            pltpu.VMEM((GROUPS, count, GW), f32),
            pltpu.VMEM((count, SSD_HEADS * HEAD_P), f32),
            dma((9,)), dma((9,)),
            dma((3,)), dma((3,)), dma((3,)), dma((3,)),
            dma((2,)), dma((2,)), dma((2,)), dma((2,)),
            dma((3,)), dma((3,)),
        ],
        compiler_params=pltpu.CompilerParams(
            collective_id=0, has_side_effects=True, vmem_limit_bytes=60 * 2**20
        ),
        name="fused_mixer_attention",
    )(q, k, v, seg, x, b, c, logs, skip, g)


def on_device(
    queries, keys, values, segment_ids, ssd_input, b_matrix, c_matrix, step_size,
    decay_log, skip_gain, cotangent,
):
    count = queries.shape[1]
    logs = step_size[0] * (-jnp.exp(decay_log))[:, None]
    skip = jnp.repeat(skip_gain, HEAD_P)[None, :]
    attention, mixed, near, far = fused(
        queries[0], keys[0], values[0], segment_ids, ssd_input[0], b_matrix[0], c_matrix[0],
        logs, skip, cotangent[0],
    )
    part = jnp.sum(near, axis=1) + jnp.sum(far.reshape(SSD_HEADS, HEAD_P), axis=1)
    grand = lax.psum(part, ("dp", "ctx"))
    decay_grad = grand / (lax.axis_size("dp") * lax.axis_size("ctx") * count)
    return attention[None], mixed[None], decay_grad


def solution(mesh):
    tok = P("dp", "ctx", None)
    return jax.shard_map(
        on_device,
        mesh=mesh,
        in_specs=(tok, tok, tok, P("dp", "ctx"), tok, tok, tok, P("dp", None, "ctx"), P(), P(), tok),
        out_specs=(tok, tok, P()),
        check_vma=False,
    )
```

```python
import functools
import functools
import math

import jax
import jax.numpy as jnp
from jax import lax
from jax.experimental import pallas as pl
from jax.experimental.pallas import tpu as pltpu
from jax.sharding import PartitionSpec as P

Q_HEADS = 32
KV_HEADS = 8
REP = Q_HEADS // KV_HEADS
WIDTH = 128
SSD_HEADS = 64
HEAD_P = 64
STATE = 128
GROUPS = 8
PER = SSD_HEADS // GROUPS
GW = PER * HEAD_P
COLS = 4
ROWS = 4
KVW = 2 * KV_HEADS * WIDTH + WIDTH
FAR_BELOW = -1e30
MESH = pl.DeviceIdType.MESH

OWN, P1, P2, AB1, AB3, AB2, BC1, BC3, BC2, RELAY = range(10)
BACK = (0, 4, 8, 1, 3, 2, 5, 7, 6)
STEP = {AB1: 1, AB2: 2, AB3: 3, BC1: 1, BC2: 2, BC3: 3}
BEFORE = {BC1: AB1, BC2: AB2, BC3: AB3}
PLAN = (
    ("P2", 1, 2, "R"), ("P1", 0), ("AB", AB1, 0, 1), ("AB", AB1, 1, 3), ("AB2", 0, 3, "D"), ("P1", 1),
    ("AB", AB1, 1, 2), ("MIX", 0), ("MIX", 1), ("AB", AB1, 1, 1), ("BC", BC3, 0, 3, "x"),
    ("P2", 1, 3, "D"), ("P2", 0, 2, "D"), ("BC", BC1, 0, 1, "z"), ("AB", AB1, 0, 0),
    ("BC", BC1, 1, 2, "z"), ("AB", AB1, 0, 2), ("AB2", 0, 2, "F"), ("AB", AB1, 1, 0), ("AB2", 1, 0, "D"),
    ("AB", AB3, 1, 1), ("ATT", OWN), ("AB", AB3, 1, 0), ("P2", 0, 3, "F"), ("AB", AB3, 1, 2),
    ("AB", AB1, 0, 3), ("BC", BC3, 0, 2, "x"), ("BC", BC2, 0, 3, "z"), ("RT", 0), ("AB2", 1, 3, "D"),
    ("RL", 1), ("BC", BC1, 1, 1, "z"), ("AB", AB3, 0, 1), ("BC", BC3, 0, 0, "x"), ("AB2", 1, 1, "M"),
    ("ENT", 0), ("BC", BC3, 1, 2, "z"), ("BC", BC2, 1, 3, "F"), ("BC", BC1, 0, 2, "x"), ("AB", AB3, 0, 2),
    ("BC", BC3, 1, 3, "x"), ("AB2", 1, 2, "F"), ("BC", BC1, 1, 3, "x"), ("BC", BC3, 1, 0, "z"),
    ("ATT", P2), ("BC", BC3, 1, 1, "z"), ("AB2", 0, 1, "F"), ("BC", BC3, 0, 1, "x"), ("AB", AB3, 1, 3),
    ("RT", 1), ("BC", BC1, 1, 0, "x"), ("BC", BC2, 0, 2, "z"), ("BC", BC1, 0, 0, "z"), ("ATT", P1),
    ("ATT", AB1), ("AB2", 0, 0, "M"), ("BC", BC1, 0, 3, "z"), ("BC", BC2, 0, 1, "z"),
    ("BC", BC2, 1, 0, "z"), ("FAR", 0), ("ENT", 1), ("BC", BC2, 0, 0, "z"), ("ATT", AB2),
    ("BC", BC2, 1, 1, "z"), ("AB", AB3, 0, 0), ("BC", BC2, 1, 2, "z"), ("AB", AB3, 0, 3), ("ATT", BC3),
    ("ATT", BC1), ("FAR", 1), ("G1",), ("ATT", BC2), ("G2",), ("ATT", AB3),
)
KEYS = KV_HEADS * WIDTH
HALVES = ((0, WIDTH + KEYS), (WIDTH + KEYS, KEYS))
ST = 2 * STATE + 16

f32, bf16 = jnp.float32, jnp.bfloat16


def dot(a, b, ca, cb, precision=None):
    return lax.dot_general(
        a, b, (((ca,), (cb,)), ((), ())), precision=precision, preferred_element_type=f32
    )


def kernel(
    q_hbm, k_hbm, v_hbm, seg_ref, x_hbm, b_hbm, c_hbm, step_ref, rate_ref, skip_ref, g_hbm,
    ao_ref, mo_ref, dg_ref, q_ref, x_ref, b_ref, c_ref, g_ref, in_sem,
    kvb, qs, acc, mrow, lrow, bias, st_own, st_row, r_out, r_in, f_out, f_in,
    d_ref, dh_ref, fexp_ref, near_ref, grad_part, g_own, g_ctx, g_dp,
    kv_ss, kv_rs, a_ss, a_rs, r_ss, r_rs, f_ss, f_rs, gc_ss, gc_rs, gd_ss, gd_rs,
):
    count = q_ref.shape[0]
    me = lax.axis_index("ctx")
    z, x = me // COLS, me % COLS

    def dev(dz, dx):
        return {"ctx": ((z + dz) % ROWS) * COLS + (x + dx) % COLS}

    def come_in(*pairs, first):
        return [
            pltpu.make_async_copy(src, to, in_sem.at[first + i]) for i, (src, to) in enumerate(pairs)
        ]

    def await_all(copies):
        for copy in copies:
            copy.wait()

    kv_in = come_in(
        (k_hbm, kvb.at[OWN, :, pl.ds(WIDTH, KEYS)]),
        (v_hbm, kvb.at[OWN, :, pl.ds(WIDTH + KEYS, KEYS)]), first=0,
    )
    mixer_in = come_in((b_hbm, b_ref), (c_hbm, c_ref), (x_hbm, x_ref), (g_hbm, g_ref), first=2)
    query_in = come_in((q_hbm, q_ref), first=6)
    for copy in kv_in + mixer_in + query_in:
        copy.start()

    n_ctx, n_dp = lax.axis_size("ctx"), lax.axis_size("dp")
    row = lax.axis_index("dp")
    barrier = pltpu.get_barrier_semaphore()

    def greet(axis, place, size):
        def one(k, _):
            to = {axis: (place + k) % size}
            pl.semaphore_signal(barrier, inc=1, device_id=to, device_id_type=MESH)
            return 0

        lax.fori_loop(1, size, one, 0)

    greet("ctx", me, n_ctx)
    greet("dp", row, n_dp)

    segrow = seg_ref[...].astype(f32)
    rr = lax.broadcasted_iota(jnp.int32, (count, count), 0)
    cc = lax.broadcasted_iota(jnp.int32, (count, count), 1)
    eye = rr == cc
    segcol = jnp.sum(jnp.where(eye, segrow, 0.0), axis=1, keepdims=True)
    lane = lax.broadcasted_iota(jnp.int32, (count, WIDTH), 1).astype(f32)
    onehot = jnp.where(lane == segcol, 1.0, 0.0).astype(bf16)
    other = jnp.where((lane != segcol) & (lane < 8.0), FAR_BELOW, 0.0).astype(bf16)
    kvb[OWN, :, :WIDTH] = other

    pl.semaphore_wait(barrier, n_ctx + n_dp - 2)
    await_all(kv_in)

    def kv_copy(src, slot, half, dz, dx, way=0):
        lanes = pl.ds(*HALVES[half])
        return pltpu.make_async_remote_copy(
            src_ref=kvb.at[src, :, lanes], dst_ref=kvb.at[slot, :, lanes],
            send_sem=kv_ss.at[slot, half, way], recv_sem=kv_rs.at[slot, half],
            device_id=dev(dz, dx), device_id_type=MESH,
        )

    sent, here, ways = [], set(), {}

    def send(when, source, slot, half, dz, dx, where):
        way = ways.get((slot, half, where), 0)
        ways[slot, half, where] = way + 1
        copy = (source, slot, half, dz, dx, way)

        @pl.when(when)
        def _():
            kv_copy(*copy).start()

        sent.append((when, copy))

    def ensure(slot, half, columns):
        todo = [k for k in columns if (slot, half, k) not in here]
        here.update((slot, half, k) for k in todo)
        if todo:
            when = me >= BACK[slot]
            if len(todo) < COLS:
                when = when & functools.reduce(jnp.logical_or, [x == k for k in todo])

            @pl.when(when)
            def _():
                kv_copy(OWN, slot, half, 0, 1).wait_recv()

    def pass_block(slot, half, to, source, start, by_z=False):
        first = -(-(BACK[slot] - to) // COLS)
        if source != OWN:
            ensure(source, half, (start,))
        if by_z:
            send((x == start) & (z >= first - 1) & (z < ROWS - 1), source, slot, half, 1, 0, start)
        else:
            send((x == start) & (z >= first), source, slot, half, 0, (to - start) % COLS, start)

    def near_block(slot, half, to, route="D"):
        if route == "D":
            pass_block(slot, half, to, P1 if to < STEP[slot] else OWN, (to - STEP[slot]) % COLS)
        else:
            back = 1 if route == "F" else -1
            pass_block(slot, half, to, AB1 if route == "F" else AB3, (to - back) % COLS)

    def far_block(slot, half, to, route):
        if route == "x":
            pass_block(slot, half, to, P2 if to < STEP[slot] else P1, (to - STEP[slot]) % COLS)
        elif route == "z":
            pass_block(slot, half, to, BEFORE[slot], to, True)
        else:
            back = 1 if route == "F" else -1
            pass_block(slot, half, to, BC1 if route == "F" else BC3, (to - back) % COLS)

    def two_back(half, to, route):
        if route == "F":
            ensure(P1, half, range(COLS))
            send(z == to - 1, P1, P2, half, 1, 0, 0)
        elif route == "D":
            send(z == to - 2, OWN, P2, half, 2, 0, 0)
        else:
            send(z == to - 2, OWN, RELAY, half, -1, 0, 0)

    def relayed(half):
        @pl.when(z == ROWS - 1)
        def _():
            kv_copy(OWN, RELAY, half, 0, 1).wait_recv()

        send(z == ROWS - 1, RELAY, P2, half, -1, 0, 0)

    mask = (cc <= rr) & (segrow == segcol)
    upper = jnp.where(rr <= cc, 1.0, 0.0)
    eyef = jnp.where(eye, 1.0, 0.0)
    keep = jnp.where(segrow == segrow[:, count - 1 : count], 1.0, 0.0)
    live = jnp.where(segrow == segrow[:, 0:1], 1.0, 0.0)
    h16 = lax.broadcasted_iota(jnp.int32, (2 * PER, GW), 0) % PER
    spread = jnp.where(h16 == lax.broadcasted_iota(jnp.int32, (2 * PER, GW), 1) // HEAD_P, 1.0, 0.0)
    spread_bf = spread.astype(bf16)
    hi = lax.Precision.HIGHEST
    low_half = lax.broadcasted_iota(jnp.int32, (count, 2 * HEAD_P), 1) < HEAD_P
    meta_rows = lax.broadcasted_iota(jnp.int32, (16, GW), 0)
    last_own, first_own = segrow[:, count - 1 : count], segrow[:, 0:1]

    def expand(value):
        top = value.astype(bf16)
        rest = (value - top.astype(f32)).astype(bf16)
        return dot(jnp.concatenate([top, rest], axis=0), spread_bf, 0, 0)

    head_rows = lax.broadcasted_iota(jnp.int32, (PER, 1), 0)

    def per_head(ref, g):
        out = jnp.zeros((PER, 1), f32)
        for j in range(PER):
            out = jnp.where(head_rows == j, ref[g * PER + j], out)
        return out

    grad_part[...] = jnp.zeros_like(grad_part)

    def pack(span, last, first):
        top = span.astype(bf16).astype(f32)
        middle = (span - top).astype(bf16).astype(f32)
        out = jnp.where(meta_rows == 0, top, jnp.where(meta_rows == 1, middle, span - top - middle))
        out = jnp.where(meta_rows == 3, last, jnp.where(meta_rows == 4, first, out))
        return out.astype(bf16)

    def unpack(block):
        m = block.astype(f32)
        return m[0:1] + m[1:2] + m[2:3], m[3:4], m[4:5]

    def mixer_group(g, _):
        cols = pl.ds(pl.multiple_of(g * GW, GW), GW)
        ncols = pl.ds(pl.multiple_of(g * STATE, STATE), STATE)
        steps = step_ref[pl.ds(pl.multiple_of(g * PER, PER), PER), :]
        cs = dot(steps, upper, 1, 0, hi) * (-jnp.exp(per_head(rate_ref, g)))
        skip_row = jnp.sum(spread[:PER] * per_head(skip_ref, g), axis=0, keepdims=True)
        cst = dot(eyef, cs, 1, 1, hi)
        span = cs[:, count - 1 : count]
        tail = span - cs
        e = jnp.exp(tail) * keep
        f = jnp.exp(cs) * live
        xg, gg = x_ref[:, cols], g_ref[:, cols]
        bg, cg = b_ref[:, ncols].astype(bf16), c_ref[:, ncols].astype(bf16)
        right = jnp.concatenate([(xg * expand(e)).astype(bf16), (xg * expand(e * tail)).astype(bf16)], axis=1)
        sh = dot(bg, right, 0, 0).astype(bf16)
        st_own[g % 2, g // 2, :STATE] = sh[:, :GW]
        st_own[g % 2, g // 2, STATE : 2 * STATE] = sh[:, GW:]
        fe = expand(f)
        fexp_ref[g] = fe
        right = jnp.concatenate([(gg * fe).astype(bf16), (gg * expand(f * cs)).astype(bf16)], axis=1)
        dd = dot(cg, right, 0, 0)
        d_ref[g] = dd[:, :GW]
        dh_ref[g] = dd[:, GW:]
        span_row = jnp.sum(spread[:PER] * span, axis=0, keepdims=True)
        st_own[g % 2, g // 2, 2 * STATE :] = pack(span_row, last_own, first_own)
        inner = dot(cg, bg, 1, 1)
        sums = []
        for pair in range(PER // 2):
            lanes = slice(pair * 2 * HEAD_P, (pair + 1) * 2 * HEAD_P)
            xp, gp = xg[:, lanes], gg[:, lanes]
            xpb, gpb = xp.astype(bf16), gp.astype(bf16)
            near = None
            for half in range(2):
                j = pair * 2 + half
                mine = low_half if half == 0 else jnp.logical_not(low_half)
                gap = jnp.where(mask, cst[:, j : j + 1] - cs[j : j + 1, :], FAR_BELOW)
                weight = jnp.exp(gap) * inner
                pairs = dot(jnp.where(mine, gpb, jnp.zeros_like(gpb)), xpb, 1, 1)
                sums.append(jnp.sum(weight * gap * pairs, axis=0, keepdims=True))
                part = dot(weight.astype(bf16), jnp.where(mine, xpb, jnp.zeros_like(xpb)), 1, 0)
                near = part if near is None else near + part
            at = pl.ds(pl.multiple_of(g * GW + pair * 2 * HEAD_P, 2 * HEAD_P), 2 * HEAD_P)
            near_ref[:, at] = near + xp * skip_row[:, lanes]
        sums = jnp.concatenate(sums, axis=0)
        rest = jnp.concatenate([sums[:, WIDTH:], jnp.zeros((PER, 2 * WIDTH - count), f32)], axis=1)
        grad_part[pl.ds(pl.multiple_of(g * PER, PER), PER), :] = sums[:, :WIDTH] + rest
        return 0

    def a_copy(c, d):
        return pltpu.make_async_remote_copy(
            src_ref=st_own.at[c, (x + d) % COLS], dst_ref=st_row.at[c, x],
            send_sem=a_ss.at[c, d - 1], recv_sem=a_rs.at[c, d - 1],
            device_id=dev(0, d), device_id_type=MESH,
        )

    def mixer_half(c):
        if c == 0:
            await_all(mixer_in)
        lax.fori_loop(0, GROUPS // 2, lambda k, u: mixer_group(2 * k + c, u), 0)
        for d in (2, 1, 3):
            a_copy(c, d).start()
        st_row[c, x] = st_own[c, x]

    scale = math.log2(math.e) / math.sqrt(WIDTH)

    def scores(slot, h):
        at = pl.ds(pl.multiple_of((1 + h) * WIDTH, WIDTH), WIDTH)
        return dot(jnp.concatenate([kvb[slot, :, at], kvb[slot, :, :WIDTH]], axis=1), qs[h], 1, 1)

    def values_of(slot, h):
        return kvb[slot, :, pl.ds(pl.multiple_of((1 + KV_HEADS + h) * WIDTH, WIDTH), WIDTH)]

    def own_head(h, _):
        s = scores(OWN, h) + bias[...]
        top = jnp.max(s, axis=0, keepdims=True)
        w = jnp.exp2((s - top) * scale)
        mrow[pl.ds(h, 1), :] = top
        lrow[pl.ds(h, 1), :] = jnp.sum(w, axis=0, keepdims=True)
        acc[h] = dot(values_of(OWN, h), w.astype(bf16), 0, 0)
        return 0

    def attend_own():
        await_all(query_in)
        for h in range(KV_HEADS):
            for r in range(REP):
                head = h * REP + r
                qs[h, r * count : (r + 1) * count, :WIDTH] = q_ref[:, head * WIDTH : (head + 1) * WIDTH]
                qs[h, r * count : (r + 1) * count, WIDTH:] = onehot
        causal = jnp.where(rr <= cc, 0.0, FAR_BELOW)
        bias[...] = jnp.concatenate([causal] * REP, axis=1)
        lax.fori_loop(0, KV_HEADS, own_head, 0)

    def attend(slot):
        def head(h, _):
            s = scores(slot, h)
            before = mrow[pl.ds(h, 1), :]
            top = jnp.maximum(before, jnp.max(s, axis=0, keepdims=True))
            w = jnp.exp2((s - top) * scale)
            fade = jnp.exp2((before - top) * scale)
            mrow[pl.ds(h, 1), :] = top
            lrow[pl.ds(h, 1), :] = lrow[pl.ds(h, 1), :] * fade + jnp.sum(w, axis=0, keepdims=True)
            acc[h] = acc[h] * fade + dot(values_of(slot, h), w.astype(bf16), 0, 0)
            return 0

        lax.fori_loop(0, KV_HEADS, head, 0)

    def states(ref, *at):
        return ref[(*at, slice(0, STATE))].astype(f32), ref[(*at, slice(STATE, 2 * STATE))].astype(f32)

    def facts(ref, *at):
        return unpack(ref[(*at, slice(2 * STATE, ST))])

    def join(s, hat, last, ref, *at):
        span, after, _ = facts(ref, *at)
        s_b, hat_b = states(ref, *at)
        fade = jnp.where(last == after, jnp.exp(span), 0.0)
        return fade * s + s_b, fade * (hat + span * s) + hat_b, after

    def r_copy(c, dz):
        return pltpu.make_async_remote_copy(
            src_ref=r_out.at[c], dst_ref=r_in.at[c, dz - 1], send_sem=r_ss.at[c, dz - 1],
            recv_sem=r_rs.at[c, dz - 1], device_id=dev(dz, 0), device_id_type=MESH,
        )

    def row_total(c):
        for d in (2, 1, 3):
            a_copy(c, d).wait_recv()
        s, hat = states(st_row, c, 0)
        total, last, _ = facts(st_row, c, 0)
        for k in range(1, COLS):
            total = total + facts(st_row, c, k)[0]
            s, hat, last = join(s, hat, last, st_row, c, k)
        r_out[c, :STATE] = s.astype(bf16)
        r_out[c, STATE : 2 * STATE] = hat.astype(bf16)
        r_out[c, 2 * STATE :] = pack(total, last, last)
        for dz in (1, 2):
            @pl.when(z + dz < ROWS)
            def _(dz=dz):
                r_copy(c, dz).start()

            @pl.when(z - dz < 0)
            def _(dz=dz):
                r_in[c, dz - 1, : 2 * STATE] = jnp.zeros((2 * STATE, GW), bf16)
                r_in[c, dz - 1, 2 * STATE :] = jnp.full((16, GW), -1.0, bf16)

    def f_copy(c, d):
        return pltpu.make_async_remote_copy(
            src_ref=f_out.at[c, (x + d) % COLS], dst_ref=f_in.at[c, x],
            send_sem=f_ss.at[c, d - 1], recv_sem=f_rs.at[c, d - 1],
            device_id=dev(0, d), device_id_type=MESH,
        )

    def entering(c):
        for dz in (1, 2):
            @pl.when(z - dz >= 0)
            def _(dz=dz):
                r_copy(c, dz).wait_recv()
        s, hat = states(r_in, c, 1)
        s, hat, last = join(s, hat, facts(r_in, c, 1)[1], r_in, c, 0)
        for k in range(COLS):
            goes_on = jnp.where(facts(st_row, c, k)[2] == last, 1.0, 0.0)
            f_out[c, k, :STATE] = (s * goes_on).astype(bf16)
            f_out[c, k, STATE:] = (hat * goes_on).astype(bf16)
            if k < COLS - 1:
                s, hat, last = join(s, hat, last, st_row, c, k)
        for d in (2, 1, 3):
            f_copy(c, d).start()
        f_in[c, x] = f_out[c, x]

    def meet(slot):
        ensure(slot, 0, range(COLS))
        ensure(slot, 1, range(COLS))

        @pl.when(me >= BACK[slot])
        def _():
            attend(slot)

    def far_group(c, k):
        g = 2 * k + c
        cols = pl.ds(pl.multiple_of(g * GW, GW), GW)
        ncols = pl.ds(pl.multiple_of(g * STATE, STATE), STATE)
        s_in, hat_in = f_in[c, k, :STATE], f_in[c, k, STATE:]
        far = dot(c_ref[:, ncols].astype(bf16), s_in, 1, 0) * fexp_ref[g]
        mo_ref[:, cols] = (near_ref[:, cols] + far).astype(bf16)
        terms = hat_in.astype(f32) * d_ref[g] + s_in.astype(f32) * dh_ref[g]
        by_head = spread[:PER] * jnp.sum(terms, axis=0, keepdims=True)
        at = pl.ds(pl.multiple_of(g * PER, PER), PER)
        grad_part[at, :] = grad_part[at, :] + sum(by_head[:, i * WIDTH : (i + 1) * WIDTH] for i in range(GW // WIDTH))
        return 0

    def far_half(c):
        for d in (2, 1, 3):
            f_copy(c, d).wait_recv()
        lax.fori_loop(0, GROUPS // 2, lambda k, _: far_group(c, k), 0)

    def gc_copy(k):
        return pltpu.make_async_remote_copy(
            src_ref=g_own.at[0], dst_ref=g_ctx.at[me], send_sem=gc_ss.at[k],
            recv_sem=gc_rs.at[k], device_id={"ctx": (me + k) % n_ctx}, device_id_type=MESH,
        )

    def gd_copy(k):
        return pltpu.make_async_remote_copy(
            src_ref=g_own.at[1], dst_ref=g_dp.at[row], send_sem=gd_ss.at[k],
            recv_sem=gd_rs.at[k], device_id={"dp": (row + k) % n_dp}, device_id_type=MESH,
        )

    def each(first, last, act):
        def one(k, _):
            act(k)
            return 0

        lax.fori_loop(first, last, one, 0)

    def window_sum():
        g_own[0] = dot(jnp.ones((8, WIDTH), f32), grad_part[...], 1, 1, hi)
        g_ctx[me] = g_own[0]
        each(1, n_ctx, lambda k: gc_copy(k).start())

    def whole_sum():
        each(1, n_ctx, lambda k: gc_copy(k).wait_recv())
        g_own[1] = lax.fori_loop(0, n_ctx, lambda k, t: t + g_ctx[k], jnp.zeros((8, WIDTH), f32))
        g_dp[row] = g_own[1]
        each(1, n_dp, lambda k: gd_copy(k).start())

    for name, *what in PLAN:
        if name == "P1":
            send(z < ROWS - 1, OWN, P1, what[0], 1, 0, 0)
        elif name == "ATT" and what[0] == OWN:
            attend_own()
        elif name == "ATT":
            meet(what[0])
        else:
            {"P2": two_back, "RL": relayed, "AB": near_block, "BC": far_block,
             "AB2": lambda half, to, route: near_block(AB2, half, to, route), "MIX": mixer_half, "RT": row_total, "ENT": entering, "FAR": far_half,
             "G1": window_sum, "G2": whole_sum}[name](*what)

    for h in range(KV_HEADS):
        out = (acc[h] / lrow[h : h + 1, :]).T.astype(bf16)
        for r in range(REP):
            head = h * REP + r
            ao_ref[:, head * WIDTH : (head + 1) * WIDTH] = out[r * count : (r + 1) * count]

    each(1, n_dp, lambda k: gd_copy(k).wait_recv())
    total = lax.fori_loop(0, n_dp, lambda k, t: t + g_dp[k], jnp.zeros((8, WIDTH), f32))
    dg_ref[...] = total * (1.0 / (n_ctx * n_dp * count))
    each(1, n_ctx, lambda k: gc_copy(k).wait_send())
    each(1, n_dp, lambda k: gd_copy(k).wait_send())

    for when, copy in sent:
        @pl.when(when)
        def _(copy=copy):
            kv_copy(*copy).wait_send()

    for c in range(2):
        for d in (1, 2, 3):
            a_copy(c, d).wait_send()
            f_copy(c, d).wait_send()
        for dz in (1, 2):
            @pl.when(z + dz < ROWS)
            def _(c=c, dz=dz):
                r_copy(c, dz).wait_send()


def fused(q, k, v, seg, x, b, c, step, rate, skip, g):
    count = q.shape[0]
    vmem = pl.BlockSpec(memory_space=pltpu.VMEM)
    smem = pl.BlockSpec(memory_space=pltpu.SMEM)
    hbm = pl.BlockSpec(memory_space=pl.ANY)
    dma = pltpu.SemaphoreType.DMA
    n_ctx, n_dp = lax.axis_size("ctx"), lax.axis_size("dp")
    return pl.pallas_call(
        kernel,
        out_shape=(
            jax.ShapeDtypeStruct((count, Q_HEADS * WIDTH), bf16),
            jax.ShapeDtypeStruct((count, SSD_HEADS * HEAD_P), bf16),
            jax.ShapeDtypeStruct((8, WIDTH), f32),
        ),
        in_specs=[hbm] * 3 + [vmem] + [hbm] * 3 + [vmem] + [smem] * 2 + [hbm],
        out_specs=(vmem,) * 3,
        scratch_shapes=[
            pltpu.VMEM((count, Q_HEADS * WIDTH), bf16),
            pltpu.VMEM((count, SSD_HEADS * HEAD_P), f32),
            pltpu.VMEM((count, GROUPS * STATE), f32),
            pltpu.VMEM((count, GROUPS * STATE), f32),
            pltpu.VMEM((count, SSD_HEADS * HEAD_P), f32),
            dma((7,)),
            pltpu.VMEM((10, count, KVW), bf16),
            pltpu.VMEM((KV_HEADS, REP * count, 2 * WIDTH), bf16),
            pltpu.VMEM((KV_HEADS, WIDTH, REP * count), f32),
            pltpu.VMEM((KV_HEADS, REP * count), f32),
            pltpu.VMEM((KV_HEADS, REP * count), f32),
            pltpu.VMEM((count, REP * count), f32),
            pltpu.VMEM((2, COLS, ST, GW), bf16),
            pltpu.VMEM((2, COLS, ST, GW), bf16),
            pltpu.VMEM((2, ST, GW), bf16),
            pltpu.VMEM((2, 2, ST, GW), bf16),
            pltpu.VMEM((2, COLS, 2 * STATE, GW), bf16),
            pltpu.VMEM((2, COLS, 2 * STATE, GW), bf16),
            pltpu.VMEM((GROUPS, STATE, GW), f32),
            pltpu.VMEM((GROUPS, STATE, GW), f32),
            pltpu.VMEM((GROUPS, count, GW), f32),
            pltpu.VMEM((count, SSD_HEADS * HEAD_P), f32),
            pltpu.VMEM((WIDTH, WIDTH), f32),
            pltpu.VMEM((2, 8, WIDTH), f32),
            pltpu.VMEM((n_ctx, 8, WIDTH), f32),
            pltpu.VMEM((n_dp, 8, WIDTH), f32),
            dma((10, 2, 4)), dma((10, 2)),
            dma((2, 3)), dma((2, 3)), dma((2, 2)), dma((2, 2)), dma((2, 3)), dma((2, 3)),
            dma((n_ctx,)), dma((n_ctx,)), dma((n_dp,)), dma((n_dp,)),
        ],
        compiler_params=pltpu.CompilerParams(
            collective_id=0, has_side_effects=True, vmem_limit_bytes=60 * 2**20
        ),
        name="fused_mixer_attention",
    )(q, k, v, seg, x, b, c, step, rate, skip, g)


def on_device(
    queries, keys, values, segment_ids, ssd_input, b_matrix, c_matrix, step_size,
    decay_log, skip_gain, cotangent,
):
    attention, mixed, decay_grad = fused(
        queries[0], keys[0], values[0], segment_ids, ssd_input[0], b_matrix[0], c_matrix[0],
        step_size[0], decay_log, skip_gain, cotangent[0],
    )
    return attention[None], mixed[None], decay_grad[0, :SSD_HEADS]


def solution(mesh):
    tok = P("dp", "ctx", None)
    return jax.shard_map(
        on_device,
        mesh=mesh,
        in_specs=(tok, tok, tok, P("dp", "ctx"), tok, tok, tok, P("dp", None, "ctx"), P(), P(), tok),
        out_specs=(tok, tok, P()),
        check_vma=False,
    )
```

```python
import functools
import functools
import math

import jax
import jax.numpy as jnp
from jax import lax
from jax.experimental import pallas as pl
from jax.experimental.pallas import tpu as pltpu
from jax.sharding import PartitionSpec as P

Q_HEADS = 32
KV_HEADS = 8
REP = Q_HEADS // KV_HEADS
WIDTH = 128
SSD_HEADS = 64
HEAD_P = 64
STATE = 128
GROUPS = 8
PER = SSD_HEADS // GROUPS
GW = PER * HEAD_P
COLS = 4
ROWS = 4
KVW = 2 * KV_HEADS * WIDTH + WIDTH
FAR_BELOW = -1e30
MESH = pl.DeviceIdType.MESH

OWN, P1, P2, AB1, AB3, AB2, BC1, BC3, BC2, RELAY = range(10)
BACK = (0, 4, 8, 1, 3, 2, 5, 7, 6)
STEP = {AB1: 1, AB2: 2, AB3: 3, BC1: 1, BC2: 2, BC3: 3}
BEFORE = {BC1: AB1, BC2: AB2, BC3: AB3}
PLAN = (
    ("AB2", 1, 3, "D"), ("P1", 0), ("P2", 0, 2, "R"), ("P2", 1, 2, "R"), ("AB", AB1, 1, 2),
    ("AB", AB1, 1, 1), ("AB", AB1, 1, 3), ("MIX", 0), ("P1", 1), ("MIX", 1), ("ATT", OWN, 0),
    ("AB", AB3, 1, 0), ("ATT", P1, 0), ("RT", 0), ("AB2", 1, 1, "D"), ("P2", 1, 3, "D"), ("AB", AB3, 1, 3),
    ("AB", AB3, 0, 2), ("AB", AB3, 0, 0), ("AB", AB3, 0, 3), ("AB", AB1, 0, 3), ("AB", AB1, 0, 0),
    ("AB", AB1, 0, 1), ("AB", AB3, 0, 1), ("AB", AB1, 0, 2), ("RT", 1), ("BC", BC1, 0, 2, "z"), ("RL", 1),
    ("AB2", 0, 1, "F"), ("AB2", 0, 2, "F"), ("BC", BC3, 0, 3, "x"), ("BC", BC1, 0, 1, "z"),
    ("BC", BC1, 1, 3, "z"), ("P2", 0, 3, "D"), ("AB", AB1, 1, 0), ("AB2", 0, 3, "F"), ("ATT", OWN, 1),
    ("AB2", 1, 0, "D"), ("AB", AB3, 1, 2), ("BC", BC1, 1, 0, "x"), ("BC", BC1, 0, 0, "z"), ("ATT", AB1, 0),
    ("BC", BC1, 1, 2, "x"), ("BC", BC1, 0, 3, "z"), ("AB2", 0, 0, "M"), ("AB", AB3, 1, 1),
    ("BC", BC3, 0, 1, "z"), ("AB2", 1, 2, "M"), ("RL", 0), ("ATT", AB3, 0), ("BC", BC3, 0, 2, "z"),
    ("ATT", P1, 1), ("BC", BC3, 1, 3, "z"), ("ENT", 0), ("ATT", AB1, 1), ("BC", BC3, 1, 2, "z"),
    ("ATT", AB3, 1), ("ENT", 1), ("BC", BC3, 0, 0, "z"), ("BC", BC3, 1, 1, "x"), ("BC", BC1, 1, 1, "z"),
    ("ATT", P2, 0), ("ATT", AB2, 0), ("BC", BC2, 0, 1, "F"), ("BC", BC2, 1, 2, "z"),
    ("BC", BC2, 1, 0, "z"), ("BC", BC3, 1, 0, "x"), ("ATT", AB2, 1), ("ATT", BC1, 0),
    ("BC", BC2, 0, 2, "F"), ("BC", BC2, 1, 3, "F"), ("BC", BC2, 0, 3, "z"), ("BC", BC2, 1, 1, "z"),
    ("BC", BC2, 0, 0, "z"), ("ATT", P2, 1), ("ATT", BC3, 0), ("ATT", BC1, 1), ("FAR", 0), ("FAR", 1),
    ("G1",), ("ATT", BC3, 1), ("ATT", BC2, 1), ("G2",), ("ATT", BC2, 0),
)
KEYS = KV_HEADS * WIDTH // 2
HALVES = ((0, WIDTH + 2 * KEYS), (WIDTH + 2 * KEYS, 2 * KEYS))
ST = 2 * STATE + 16

f32, bf16 = jnp.float32, jnp.bfloat16


def dot(a, b, ca, cb, precision=None):
    return lax.dot_general(
        a, b, (((ca,), (cb,)), ((), ())), precision=precision, preferred_element_type=f32
    )


def kernel(
    q_hbm, k_hbm, v_hbm, seg_ref, x_hbm, b_hbm, c_hbm, step_ref, rate_ref, skip_ref, g_hbm,
    ao_ref, mo_ref, dg_ref, q_ref, x_ref, b_ref, c_ref, g_ref, in_sem,
    kvb, qs, acc, mrow, lrow, bias, st_own, st_row, r_out, r_in, f_out, f_in,
    d_ref, dh_ref, fexp_ref, near_ref, grad_part, g_own, g_ctx, g_dp,
    kv_ss, kv_rs, a_ss, a_rs, r_ss, r_rs, f_ss, f_rs, gc_ss, gc_rs, gd_ss, gd_rs,
):
    count = q_ref.shape[0]
    me = lax.axis_index("ctx")
    z, x = me // COLS, me % COLS

    def dev(dz, dx):
        return {"ctx": ((z + dz) % ROWS) * COLS + (x + dx) % COLS}

    def come_in(*pairs, first):
        return [
            pltpu.make_async_copy(src, to, in_sem.at[first + i]) for i, (src, to) in enumerate(pairs)
        ]

    def await_all(copies):
        for copy in copies:
            copy.wait()

    kv_in = come_in(
        *(
            (src.at[:, pl.ds(half * KEYS, KEYS)], kvb.at[OWN, :, pl.ds(WIDTH + (2 * half + i) * KEYS, KEYS)])
            for half in (0, 1) for i, src in enumerate((k_hbm, v_hbm))
        ), first=0,
    )
    mixer_in = come_in((b_hbm, b_ref), (c_hbm, c_ref), (x_hbm, x_ref), (g_hbm, g_ref), first=4)
    query_in = come_in((q_hbm, q_ref), first=8)
    for copy in kv_in + mixer_in + query_in:
        copy.start()

    n_ctx, n_dp = lax.axis_size("ctx"), lax.axis_size("dp")
    row = lax.axis_index("dp")
    barrier = pltpu.get_barrier_semaphore()

    def greet(axis, place, size):
        def one(k, _):
            to = {axis: (place + k) % size}
            pl.semaphore_signal(barrier, inc=1, device_id=to, device_id_type=MESH)
            return 0

        lax.fori_loop(1, size, one, 0)

    greet("ctx", me, n_ctx)
    greet("dp", row, n_dp)

    segrow = seg_ref[...].astype(f32)
    rr = lax.broadcasted_iota(jnp.int32, (count, count), 0)
    cc = lax.broadcasted_iota(jnp.int32, (count, count), 1)
    eye = rr == cc
    segcol = jnp.sum(jnp.where(eye, segrow, 0.0), axis=1, keepdims=True)
    lane = lax.broadcasted_iota(jnp.int32, (count, WIDTH), 1).astype(f32)
    onehot = jnp.where(lane == segcol, 1.0, 0.0).astype(bf16)
    other = jnp.where((lane != segcol) & (lane < 8.0), FAR_BELOW, 0.0).astype(bf16)
    kvb[OWN, :, :WIDTH] = other

    pl.semaphore_wait(barrier, n_ctx + n_dp - 2)
    await_all(kv_in)

    def kv_copy(src, slot, half, dz, dx, way=0):
        lanes = pl.ds(*HALVES[half])
        return pltpu.make_async_remote_copy(
            src_ref=kvb.at[src, :, lanes], dst_ref=kvb.at[slot, :, lanes],
            send_sem=kv_ss.at[slot, half, way], recv_sem=kv_rs.at[slot, half],
            device_id=dev(dz, dx), device_id_type=MESH,
        )

    sent, here, ways = [], set(), {}

    def send(when, source, slot, half, dz, dx, where):
        way = ways.get((slot, half, where), 0)
        ways[slot, half, where] = way + 1
        copy = (source, slot, half, dz, dx, way)

        @pl.when(when)
        def _():
            kv_copy(*copy).start()

        sent.append((when, copy))

    def ensure(slot, half, columns):
        todo = [k for k in columns if (slot, half, k) not in here]
        here.update((slot, half, k) for k in todo)
        if todo:
            when = me >= BACK[slot]
            if len(todo) < COLS:
                when = when & functools.reduce(jnp.logical_or, [x == k for k in todo])

            @pl.when(when)
            def _():
                kv_copy(OWN, slot, half, 0, 1).wait_recv()

    def pass_block(slot, half, to, source, start, by_z=False):
        first = -(-(BACK[slot] - to) // COLS)
        if source != OWN:
            ensure(source, half, (start,))
        if by_z:
            send((x == start) & (z >= first - 1) & (z < ROWS - 1), source, slot, half, 1, 0, start)
        else:
            send((x == start) & (z >= first), source, slot, half, 0, (to - start) % COLS, start)

    def near_block(slot, half, to, route="D"):
        if route == "D":
            pass_block(slot, half, to, P1 if to < STEP[slot] else OWN, (to - STEP[slot]) % COLS)
        else:
            back = 1 if route == "F" else -1
            pass_block(slot, half, to, AB1 if route == "F" else AB3, (to - back) % COLS)

    def far_block(slot, half, to, route):
        if route == "x":
            pass_block(slot, half, to, P2 if to < STEP[slot] else P1, (to - STEP[slot]) % COLS)
        elif route == "z":
            pass_block(slot, half, to, BEFORE[slot], to, True)
        else:
            back = 1 if route == "F" else -1
            pass_block(slot, half, to, BC1 if route == "F" else BC3, (to - back) % COLS)

    def two_back(half, to, route):
        if route == "F":
            ensure(P1, half, range(COLS))
            send(z == to - 1, P1, P2, half, 1, 0, 0)
        elif route == "D":
            send(z == to - 2, OWN, P2, half, 2, 0, 0)
        else:
            send(z == to - 2, OWN, RELAY, half, -1, 0, 0)

    def relayed(half):
        @pl.when(z == ROWS - 1)
        def _():
            kv_copy(OWN, RELAY, half, 0, 1).wait_recv()

        send(z == ROWS - 1, RELAY, P2, half, -1, 0, 0)

    mask = (cc <= rr) & (segrow == segcol)
    upper = jnp.where(rr <= cc, 1.0, 0.0)
    eyef = jnp.where(eye, 1.0, 0.0)
    keep = jnp.where(segrow == segrow[:, count - 1 : count], 1.0, 0.0)
    live = jnp.where(segrow == segrow[:, 0:1], 1.0, 0.0)
    h16 = lax.broadcasted_iota(jnp.int32, (2 * PER, GW), 0) % PER
    spread = jnp.where(h16 == lax.broadcasted_iota(jnp.int32, (2 * PER, GW), 1) // HEAD_P, 1.0, 0.0)
    spread_bf = spread.astype(bf16)
    hi = lax.Precision.HIGHEST
    low_half = lax.broadcasted_iota(jnp.int32, (count, 2 * HEAD_P), 1) < HEAD_P
    meta_rows = lax.broadcasted_iota(jnp.int32, (16, GW), 0)
    last_own, first_own = segrow[:, count - 1 : count], segrow[:, 0:1]

    def expand(value):
        top = value.astype(bf16)
        rest = (value - top.astype(f32)).astype(bf16)
        return dot(jnp.concatenate([top, rest], axis=0), spread_bf, 0, 0)

    head_rows = lax.broadcasted_iota(jnp.int32, (PER, 1), 0)

    def per_head(ref, g):
        out = jnp.zeros((PER, 1), f32)
        for j in range(PER):
            out = jnp.where(head_rows == j, ref[g * PER + j], out)
        return out

    grad_part[...] = jnp.zeros_like(grad_part)

    def pack(span, last, first):
        top = span.astype(bf16).astype(f32)
        middle = (span - top).astype(bf16).astype(f32)
        out = jnp.where(meta_rows == 0, top, jnp.where(meta_rows == 1, middle, span - top - middle))
        out = jnp.where(meta_rows == 3, last, jnp.where(meta_rows == 4, first, out))
        return out.astype(bf16)

    def unpack(block):
        m = block.astype(f32)
        return m[0:1] + m[1:2] + m[2:3], m[3:4], m[4:5]

    def mixer_group(g, _):
        cols = pl.ds(pl.multiple_of(g * GW, GW), GW)
        ncols = pl.ds(pl.multiple_of(g * STATE, STATE), STATE)
        steps = step_ref[pl.ds(pl.multiple_of(g * PER, PER), PER), :]
        cs = dot(steps, upper, 1, 0, hi) * (-jnp.exp(per_head(rate_ref, g)))
        skip_row = jnp.sum(spread[:PER] * per_head(skip_ref, g), axis=0, keepdims=True)
        cst = dot(eyef, cs, 1, 1, hi)
        span = cs[:, count - 1 : count]
        tail = span - cs
        e = jnp.exp(tail) * keep
        f = jnp.exp(cs) * live
        xg, gg = x_ref[:, cols], g_ref[:, cols]
        bg, cg = b_ref[:, ncols].astype(bf16), c_ref[:, ncols].astype(bf16)
        right = jnp.concatenate([(xg * expand(e)).astype(bf16), (xg * expand(e * tail)).astype(bf16)], axis=1)
        sh = dot(bg, right, 0, 0).astype(bf16)
        st_own[g % 2, g // 2, :STATE] = sh[:, :GW]
        st_own[g % 2, g // 2, STATE : 2 * STATE] = sh[:, GW:]
        fe = expand(f)
        fexp_ref[g] = fe
        right = jnp.concatenate([(gg * fe).astype(bf16), (gg * expand(f * cs)).astype(bf16)], axis=1)
        dd = dot(cg, right, 0, 0)
        d_ref[g] = dd[:, :GW]
        dh_ref[g] = dd[:, GW:]
        span_row = jnp.sum(spread[:PER] * span, axis=0, keepdims=True)
        st_own[g % 2, g // 2, 2 * STATE :] = pack(span_row, last_own, first_own)
        inner = dot(cg, bg, 1, 1)
        sums = []
        for pair in range(PER // 2):
            lanes = slice(pair * 2 * HEAD_P, (pair + 1) * 2 * HEAD_P)
            xp, gp = xg[:, lanes], gg[:, lanes]
            xpb, gpb = xp.astype(bf16), gp.astype(bf16)
            near = None
            for half in range(2):
                j = pair * 2 + half
                mine = low_half if half == 0 else jnp.logical_not(low_half)
                gap = jnp.where(mask, cst[:, j : j + 1] - cs[j : j + 1, :], FAR_BELOW)
                weight = jnp.exp(gap) * inner
                pairs = dot(jnp.where(mine, gpb, jnp.zeros_like(gpb)), xpb, 1, 1)
                sums.append(jnp.sum(weight * gap * pairs, axis=0, keepdims=True))
                part = dot(weight.astype(bf16), jnp.where(mine, xpb, jnp.zeros_like(xpb)), 1, 0)
                near = part if near is None else near + part
            at = pl.ds(pl.multiple_of(g * GW + pair * 2 * HEAD_P, 2 * HEAD_P), 2 * HEAD_P)
            near_ref[:, at] = near + xp * skip_row[:, lanes]
        sums = jnp.concatenate(sums, axis=0)
        rest = jnp.concatenate([sums[:, WIDTH:], jnp.zeros((PER, 2 * WIDTH - count), f32)], axis=1)
        grad_part[pl.ds(pl.multiple_of(g * PER, PER), PER), :] = sums[:, :WIDTH] + rest
        return 0

    def a_copy(c, d):
        return pltpu.make_async_remote_copy(
            src_ref=st_own.at[c, (x + d) % COLS], dst_ref=st_row.at[c, x],
            send_sem=a_ss.at[c, d - 1], recv_sem=a_rs.at[c, d - 1],
            device_id=dev(0, d), device_id_type=MESH,
        )

    def mixer_half(c):
        if c == 0:
            await_all(mixer_in)
        lax.fori_loop(0, GROUPS // 2, lambda k, u: mixer_group(2 * k + c, u), 0)
        for d in (2, 1, 3):
            a_copy(c, d).start()
        st_row[c, x] = st_own[c, x]

    scale = math.log2(math.e) / math.sqrt(WIDTH)

    def lanes_of(h, which):
        at = WIDTH + (2 * (h // (KV_HEADS // 2)) + which) * KEYS + (h % (KV_HEADS // 2)) * WIDTH
        return pl.ds(pl.multiple_of(at, WIDTH), WIDTH)

    def scores(slot, h):
        keys = kvb[slot, :, lanes_of(h, 0)]
        return dot(jnp.concatenate([keys, kvb[slot, :, :WIDTH]], axis=1), qs[h], 1, 1)

    def values_of(slot, h):
        return kvb[slot, :, lanes_of(h, 1)]

    def own_head(h, _):
        s = scores(OWN, h) + bias[...]
        top = jnp.max(s, axis=0, keepdims=True)
        w = jnp.exp2((s - top) * scale)
        mrow[pl.ds(h, 1), :] = top
        lrow[pl.ds(h, 1), :] = jnp.sum(w, axis=0, keepdims=True)
        acc[h] = dot(values_of(OWN, h), w.astype(bf16), 0, 0)
        return 0

    def heads_of(half):
        return half * KV_HEADS // 2, (half + 1) * KV_HEADS // 2

    causal = jnp.where(rr <= cc, 0.0, FAR_BELOW)
    bias[...] = jnp.concatenate([causal] * REP, axis=1)

    def attend_own(half):
        if half == 0:
            await_all(query_in)
        for h in range(*heads_of(half)):
            for r in range(REP):
                head = h * REP + r
                qs[h, r * count : (r + 1) * count, :WIDTH] = q_ref[:, head * WIDTH : (head + 1) * WIDTH]
                qs[h, r * count : (r + 1) * count, WIDTH:] = onehot
        lax.fori_loop(*heads_of(half), own_head, 0)

    def attend(slot, half):
        def head(h, _):
            s = scores(slot, h)
            before = mrow[pl.ds(h, 1), :]
            top = jnp.maximum(before, jnp.max(s, axis=0, keepdims=True))
            w = jnp.exp2((s - top) * scale)
            fade = jnp.exp2((before - top) * scale)
            mrow[pl.ds(h, 1), :] = top
            lrow[pl.ds(h, 1), :] = lrow[pl.ds(h, 1), :] * fade + jnp.sum(w, axis=0, keepdims=True)
            acc[h] = acc[h] * fade + dot(values_of(slot, h), w.astype(bf16), 0, 0)
            return 0

        lax.fori_loop(*heads_of(half), head, 0)

    def states(ref, *at):
        return ref[(*at, slice(0, STATE))].astype(f32), ref[(*at, slice(STATE, 2 * STATE))].astype(f32)

    def facts(ref, *at):
        return unpack(ref[(*at, slice(2 * STATE, ST))])

    def join(s, hat, last, ref, *at):
        span, after, _ = facts(ref, *at)
        s_b, hat_b = states(ref, *at)
        fade = jnp.where(last == after, jnp.exp(span), 0.0)
        return fade * s + s_b, fade * (hat + span * s) + hat_b, after

    def r_copy(c, dz):
        return pltpu.make_async_remote_copy(
            src_ref=r_out.at[c], dst_ref=r_in.at[c, dz - 1], send_sem=r_ss.at[c, dz - 1],
            recv_sem=r_rs.at[c, dz - 1], device_id=dev(dz, 0), device_id_type=MESH,
        )

    def row_total(c):
        for d in (2, 1, 3):
            a_copy(c, d).wait_recv()
        s, hat = states(st_row, c, 0)
        total, last, _ = facts(st_row, c, 0)
        for k in range(1, COLS):
            total = total + facts(st_row, c, k)[0]
            s, hat, last = join(s, hat, last, st_row, c, k)
        r_out[c, :STATE] = s.astype(bf16)
        r_out[c, STATE : 2 * STATE] = hat.astype(bf16)
        r_out[c, 2 * STATE :] = pack(total, last, last)
        for dz in (1, 2):
            @pl.when(z + dz < ROWS)
            def _(dz=dz):
                r_copy(c, dz).start()

            @pl.when(z - dz < 0)
            def _(dz=dz):
                r_in[c, dz - 1, : 2 * STATE] = jnp.zeros((2 * STATE, GW), bf16)
                r_in[c, dz - 1, 2 * STATE :] = jnp.full((16, GW), -1.0, bf16)

    def f_copy(c, d):
        return pltpu.make_async_remote_copy(
            src_ref=f_out.at[c, (x + d) % COLS], dst_ref=f_in.at[c, x],
            send_sem=f_ss.at[c, d - 1], recv_sem=f_rs.at[c, d - 1],
            device_id=dev(0, d), device_id_type=MESH,
        )

    def entering(c):
        for dz in (1, 2):
            @pl.when(z - dz >= 0)
            def _(dz=dz):
                r_copy(c, dz).wait_recv()
        s, hat = states(r_in, c, 1)
        s, hat, last = join(s, hat, facts(r_in, c, 1)[1], r_in, c, 0)
        for k in range(COLS):
            goes_on = jnp.where(facts(st_row, c, k)[2] == last, 1.0, 0.0)
            f_out[c, k, :STATE] = (s * goes_on).astype(bf16)
            f_out[c, k, STATE:] = (hat * goes_on).astype(bf16)
            if k < COLS - 1:
                s, hat, last = join(s, hat, last, st_row, c, k)
        for d in (2, 1, 3):
            f_copy(c, d).start()
        f_in[c, x] = f_out[c, x]

    def meet(slot, half):
        ensure(slot, 0, range(COLS))
        if half == 1:
            ensure(slot, 1, range(COLS))

        @pl.when(me >= BACK[slot])
        def _():
            attend(slot, half)

    def far_group(c, k):
        g = 2 * k + c
        cols = pl.ds(pl.multiple_of(g * GW, GW), GW)
        ncols = pl.ds(pl.multiple_of(g * STATE, STATE), STATE)
        s_in, hat_in = f_in[c, k, :STATE], f_in[c, k, STATE:]
        far = dot(c_ref[:, ncols].astype(bf16), s_in, 1, 0) * fexp_ref[g]
        mo_ref[:, cols] = (near_ref[:, cols] + far).astype(bf16)
        terms = hat_in.astype(f32) * d_ref[g] + s_in.astype(f32) * dh_ref[g]
        by_head = spread[:PER] * jnp.sum(terms, axis=0, keepdims=True)
        at = pl.ds(pl.multiple_of(g * PER, PER), PER)
        grad_part[at, :] = grad_part[at, :] + sum(by_head[:, i * WIDTH : (i + 1) * WIDTH] for i in range(GW // WIDTH))
        return 0

    def far_half(c):
        for d in (2, 1, 3):
            f_copy(c, d).wait_recv()
        lax.fori_loop(0, GROUPS // 2, lambda k, _: far_group(c, k), 0)

    def gc_copy(k):
        return pltpu.make_async_remote_copy(
            src_ref=g_own.at[0], dst_ref=g_ctx.at[me], send_sem=gc_ss.at[k],
            recv_sem=gc_rs.at[k], device_id={"ctx": (me + k) % n_ctx}, device_id_type=MESH,
        )

    def gd_copy(k):
        return pltpu.make_async_remote_copy(
            src_ref=g_own.at[1], dst_ref=g_dp.at[row], send_sem=gd_ss.at[k],
            recv_sem=gd_rs.at[k], device_id={"dp": (row + k) % n_dp}, device_id_type=MESH,
        )

    def each(first, last, act):
        def one(k, _):
            act(k)
            return 0

        lax.fori_loop(first, last, one, 0)

    def window_sum():
        g_own[0] = dot(jnp.ones((8, WIDTH), f32), grad_part[...], 1, 1, hi)
        g_ctx[me] = g_own[0]
        each(1, n_ctx, lambda k: gc_copy(k).start())

    def whole_sum():
        each(1, n_ctx, lambda k: gc_copy(k).wait_recv())
        g_own[1] = lax.fori_loop(0, n_ctx, lambda k, t: t + g_ctx[k], jnp.zeros((8, WIDTH), f32))
        g_dp[row] = g_own[1]
        each(1, n_dp, lambda k: gd_copy(k).start())

    for name, *what in PLAN:
        if name == "P1":
            send(z < ROWS - 1, OWN, P1, what[0], 1, 0, 0)
        elif name == "ATT" and what[0] == OWN:
            attend_own(what[1])
        elif name == "ATT":
            meet(*what)
        else:
            {"P2": two_back, "RL": relayed, "AB": near_block, "BC": far_block,
             "AB2": lambda half, to, route: near_block(AB2, half, to, route), "MIX": mixer_half, "RT": row_total, "ENT": entering, "FAR": far_half,
             "G1": window_sum, "G2": whole_sum}[name](*what)

    for h in range(KV_HEADS):
        out = (acc[h] / lrow[h : h + 1, :]).T.astype(bf16)
        for r in range(REP):
            head = h * REP + r
            ao_ref[:, head * WIDTH : (head + 1) * WIDTH] = out[r * count : (r + 1) * count]

    each(1, n_dp, lambda k: gd_copy(k).wait_recv())
    total = lax.fori_loop(0, n_dp, lambda k, t: t + g_dp[k], jnp.zeros((8, WIDTH), f32))
    dg_ref[...] = total * (1.0 / (n_ctx * n_dp * count))
    each(1, n_ctx, lambda k: gc_copy(k).wait_send())
    each(1, n_dp, lambda k: gd_copy(k).wait_send())

    for when, copy in sent:
        @pl.when(when)
        def _(copy=copy):
            kv_copy(*copy).wait_send()

    for c in range(2):
        for d in (1, 2, 3):
            a_copy(c, d).wait_send()
            f_copy(c, d).wait_send()
        for dz in (1, 2):
            @pl.when(z + dz < ROWS)
            def _(c=c, dz=dz):
                r_copy(c, dz).wait_send()


def fused(q, k, v, seg, x, b, c, step, rate, skip, g):
    count = q.shape[0]
    vmem = pl.BlockSpec(memory_space=pltpu.VMEM)
    smem = pl.BlockSpec(memory_space=pltpu.SMEM)
    hbm = pl.BlockSpec(memory_space=pl.ANY)
    dma = pltpu.SemaphoreType.DMA
    n_ctx, n_dp = lax.axis_size("ctx"), lax.axis_size("dp")
    return pl.pallas_call(
        kernel,
        out_shape=(
            jax.ShapeDtypeStruct((count, Q_HEADS * WIDTH), bf16),
            jax.ShapeDtypeStruct((count, SSD_HEADS * HEAD_P), bf16),
            jax.ShapeDtypeStruct((8, WIDTH), f32),
        ),
        in_specs=[hbm] * 3 + [vmem] + [hbm] * 3 + [vmem] + [smem] * 2 + [hbm],
        out_specs=(vmem,) * 3,
        scratch_shapes=[
            pltpu.VMEM((count, Q_HEADS * WIDTH), bf16),
            pltpu.VMEM((count, SSD_HEADS * HEAD_P), f32),
            pltpu.VMEM((count, GROUPS * STATE), f32),
            pltpu.VMEM((count, GROUPS * STATE), f32),
            pltpu.VMEM((count, SSD_HEADS * HEAD_P), f32),
            dma((9,)),
            pltpu.VMEM((10, count, KVW), bf16),
            pltpu.VMEM((KV_HEADS, REP * count, 2 * WIDTH), bf16),
            pltpu.VMEM((KV_HEADS, WIDTH, REP * count), f32),
            pltpu.VMEM((KV_HEADS, REP * count), f32),
            pltpu.VMEM((KV_HEADS, REP * count), f32),
            pltpu.VMEM((count, REP * count), f32),
            pltpu.VMEM((2, COLS, ST, GW), bf16),
            pltpu.VMEM((2, COLS, ST, GW), bf16),
            pltpu.VMEM((2, ST, GW), bf16),
            pltpu.VMEM((2, 2, ST, GW), bf16),
            pltpu.VMEM((2, COLS, 2 * STATE, GW), bf16),
            pltpu.VMEM((2, COLS, 2 * STATE, GW), bf16),
            pltpu.VMEM((GROUPS, STATE, GW), f32),
            pltpu.VMEM((GROUPS, STATE, GW), f32),
            pltpu.VMEM((GROUPS, count, GW), f32),
            pltpu.VMEM((count, SSD_HEADS * HEAD_P), f32),
            pltpu.VMEM((WIDTH, WIDTH), f32),
            pltpu.VMEM((2, 8, WIDTH), f32),
            pltpu.VMEM((n_ctx, 8, WIDTH), f32),
            pltpu.VMEM((n_dp, 8, WIDTH), f32),
            dma((10, 2, 4)), dma((10, 2)),
            dma((2, 3)), dma((2, 3)), dma((2, 2)), dma((2, 2)), dma((2, 3)), dma((2, 3)),
            dma((n_ctx,)), dma((n_ctx,)), dma((n_dp,)), dma((n_dp,)),
        ],
        compiler_params=pltpu.CompilerParams(
            collective_id=0, has_side_effects=True, vmem_limit_bytes=60 * 2**20
        ),
        name="fused_mixer_attention",
    )(q, k, v, seg, x, b, c, step, rate, skip, g)


def on_device(
    queries, keys, values, segment_ids, ssd_input, b_matrix, c_matrix, step_size,
    decay_log, skip_gain, cotangent,
):
    attention, mixed, decay_grad = fused(
        queries[0], keys[0], values[0], segment_ids, ssd_input[0], b_matrix[0], c_matrix[0],
        step_size[0], decay_log, skip_gain, cotangent[0],
    )
    return attention[None], mixed[None], decay_grad[0, :SSD_HEADS]


def solution(mesh):
    tok = P("dp", "ctx", None)
    return jax.shard_map(
        on_device,
        mesh=mesh,
        in_specs=(tok, tok, tok, P("dp", "ctx"), tok, tok, tok, P("dp", None, "ctx"), P(), P(), tok),
        out_specs=(tok, tok, P()),
        check_vma=False,
    )
```

```python
import functools
import functools
import math

import jax
import jax.numpy as jnp
from jax import lax
from jax.experimental import pallas as pl
from jax.experimental.pallas import tpu as pltpu
from jax.sharding import PartitionSpec as P

Q_HEADS = 32
KV_HEADS = 8
REP = Q_HEADS // KV_HEADS
WIDTH = 128
SSD_HEADS = 64
HEAD_P = 64
STATE = 128
GROUPS = 8
PER = SSD_HEADS // GROUPS
GW = PER * HEAD_P
COLS = 4
ROWS = 4
KVW = 2 * KV_HEADS * WIDTH + WIDTH
FAR_BELOW = -1e30
MESH = pl.DeviceIdType.MESH

OWN, P1, P2, AB1, AB3, AB2, BC1, BC3, BC2, RELAY = range(10)
BACK = (0, 4, 8, 1, 3, 2, 5, 7, 6)
STEP = {AB1: 1, AB2: 2, AB3: 3, BC1: 1, BC2: 2, BC3: 3}
BEFORE = {BC1: AB1, BC2: AB2, BC3: AB3}
PLAN = (
    ("P2", 0, 3, "D"), ("AB", AB1, 1, 2), ("AB", AB1, 0, 1), ("AB2", 0, 3, "D"), ("P1", 1),
    ("AB", AB1, 0, 3), ("P1", 0), ("MIX", 0), ("P2", 1, 3, "D"), ("MIX", 1), ("P2", 1, 2, "F"),
    ("ATT", OWN, 0), ("P2", 0, 2, "R"), ("AB", AB1, 0, 0), ("BC", BC1, 0, 1, "z"), ("ATT", P1, 0),
    ("BC", BC1, 1, 2, "z"), ("AB", AB3, 0, 3), ("BC", BC1, 0, 3, "z"), ("AB", AB3, 1, 0),
    ("AB", AB1, 0, 2), ("ATT", OWN, 1), ("AB", AB3, 1, 3), ("AB", AB1, 1, 1), ("AB", AB3, 0, 2),
    ("AB", AB3, 0, 1), ("AB", AB3, 0, 0), ("AB", AB3, 1, 2), ("AB2", 1, 3, "F"), ("AB", AB1, 1, 3),
    ("RT", 0), ("RL", 0), ("AB2", 0, 2, "F"), ("RT", 1), ("AB2", 0, 0, "M"), ("AB", AB1, 1, 0),
    ("BC", BC1, 1, 1, "x"), ("BC", BC1, 1, 3, "x"), ("AB", AB3, 1, 1), ("ATT", P1, 1), ("ATT", P2, 1),
    ("AB2", 1, 1, "M"), ("BC", BC3, 0, 2, "x"), ("BC", BC3, 0, 3, "x"), ("AB2", 1, 2, "F"),
    ("BC", BC1, 0, 0, "z"), ("AB2", 0, 1, "F"), ("BC", BC1, 1, 0, "x"), ("ATT", AB3, 1),
    ("BC", BC3, 1, 3, "z"), ("BC", BC2, 1, 3, "z"), ("ENT", 0), ("ATT", AB1, 0), ("BC", BC3, 0, 0, "z"),
    ("BC", BC1, 0, 2, "z"), ("BC", BC3, 0, 1, "z"), ("ATT", AB3, 0), ("ATT", AB1, 1),
    ("BC", BC3, 1, 1, "z"), ("ENT", 1), ("BC", BC3, 1, 0, "z"), ("ATT", BC1, 1), ("BC", BC2, 0, 1, "M"),
    ("BC", BC3, 1, 2, "z"), ("AB2", 1, 0, "M"), ("ATT", BC1, 0), ("ATT", AB2, 0), ("ATT", P2, 0),
    ("BC", BC2, 1, 1, "F"), ("BC", BC2, 0, 3, "z"), ("FAR", 0), ("BC", BC2, 1, 0, "x"),
    ("BC", BC2, 1, 2, "F"), ("BC", BC2, 0, 2, "z"), ("BC", BC2, 0, 0, "z"), ("ATT", BC3, 0),
    ("ATT", BC3, 1), ("FAR", 1), ("G1",), ("ATT", AB2, 1), ("G2",), ("ATT", BC2, 0), ("ATT", BC2, 1),
)
KEYS = KV_HEADS * WIDTH // 2
HALVES = ((0, WIDTH + 2 * KEYS), (WIDTH + 2 * KEYS, 2 * KEYS))
ST = 2 * STATE + 16
PIECES = 6

f32, bf16 = jnp.float32, jnp.bfloat16


def dot(a, b, ca, cb, precision=None):
    return lax.dot_general(
        a, b, (((ca,), (cb,)), ((), ())), precision=precision, preferred_element_type=f32
    )


def kernel(
    q_hbm, k_hbm, v_hbm, seg_ref, x_hbm, b_hbm, c_hbm, step_ref, rate_ref, skip_ref, g_hbm,
    ao_hbm, mo_hbm, dg_ref, ao_ref, mo_ref, q_ref, x_ref, b_ref, c_ref, g_ref, in_sem, out_sem,
    kvb, qs, acc, mrow, lrow, bias, st_own, st_row, r_out, r_in, f_out, f_in,
    d_ref, dh_ref, fexp_ref, near_ref, grad_part, g_own, g_ctx, g_dp,
    kv_ss, kv_rs, a_ss, a_rs, r_ss, r_rs, f_ss, f_rs, gc_ss, gc_rs, gd_ss, gd_rs,
):
    count = q_ref.shape[0]
    me = lax.axis_index("ctx")
    z, x = me // COLS, me % COLS

    def dev(dz, dx):
        return {"ctx": ((z + dz) % ROWS) * COLS + (x + dx) % COLS}

    def come_in(*pairs, first):
        return [
            pltpu.make_async_copy(src, to, in_sem.at[first + i]) for i, (src, to) in enumerate(pairs)
        ]

    def await_all(copies):
        for copy in copies:
            copy.wait()

    kv_in = come_in(
        *(
            (src.at[:, pl.ds(half * KEYS, KEYS)], kvb.at[OWN, :, pl.ds(WIDTH + (2 * half + i) * KEYS, KEYS)])
            for half in (0, 1) for i, src in enumerate((k_hbm, v_hbm))
        ), first=0,
    )
    mixer_in = come_in((b_hbm, b_ref), (c_hbm, c_ref), (x_hbm, x_ref), (g_hbm, g_ref), first=4)
    query_in = come_in((q_hbm, q_ref), first=8)
    for copy in kv_in + mixer_in + query_in:
        copy.start()

    n_ctx, n_dp = lax.axis_size("ctx"), lax.axis_size("dp")
    row = lax.axis_index("dp")
    barrier = pltpu.get_barrier_semaphore()

    def greet(axis, place, size):
        def one(k, _):
            to = {axis: (place + k) % size}
            pl.semaphore_signal(barrier, inc=1, device_id=to, device_id_type=MESH)
            return 0

        lax.fori_loop(1, size, one, 0)

    greet("ctx", me, n_ctx)
    greet("dp", row, n_dp)

    segrow = seg_ref[...].astype(f32)
    rr = lax.broadcasted_iota(jnp.int32, (count, count), 0)
    cc = lax.broadcasted_iota(jnp.int32, (count, count), 1)
    eye = rr == cc
    segcol = jnp.sum(jnp.where(eye, segrow, 0.0), axis=1, keepdims=True)
    lane = lax.broadcasted_iota(jnp.int32, (count, WIDTH), 1).astype(f32)
    onehot = jnp.where(lane == segcol, 1.0, 0.0).astype(bf16)
    other = jnp.where((lane != segcol) & (lane < 8.0), FAR_BELOW, 0.0).astype(bf16)
    kvb[OWN, :, :WIDTH] = other

    pl.semaphore_wait(barrier, n_ctx + n_dp - 2)
    await_all(kv_in)

    def kv_copy(src, slot, half, dz, dx, way=0):
        lanes = pl.ds(*HALVES[half])
        return pltpu.make_async_remote_copy(
            src_ref=kvb.at[src, :, lanes], dst_ref=kvb.at[slot, :, lanes],
            send_sem=kv_ss.at[slot, half, way], recv_sem=kv_rs.at[slot, half],
            device_id=dev(dz, dx), device_id_type=MESH,
        )

    sent, here, ways = [], set(), {}

    def send(when, source, slot, half, dz, dx, where):
        way = ways.get((slot, half, where), 0)
        ways[slot, half, where] = way + 1
        copy = (source, slot, half, dz, dx, way)

        @pl.when(when)
        def _():
            kv_copy(*copy).start()

        sent.append((when, copy))

    def ensure(slot, half, columns):
        todo = [k for k in columns if (slot, half, k) not in here]
        here.update((slot, half, k) for k in todo)
        if todo:
            when = me >= BACK[slot]
            if len(todo) < COLS:
                when = when & functools.reduce(jnp.logical_or, [x == k for k in todo])

            @pl.when(when)
            def _():
                kv_copy(OWN, slot, half, 0, 1).wait_recv()

    def pass_block(slot, half, to, source, start, by_z=False):
        first = -(-(BACK[slot] - to) // COLS)
        if source != OWN:
            ensure(source, half, (start,))
        if by_z:
            send((x == start) & (z >= first - 1) & (z < ROWS - 1), source, slot, half, 1, 0, start)
        else:
            send((x == start) & (z >= first), source, slot, half, 0, (to - start) % COLS, start)

    def near_block(slot, half, to, route="D"):
        if route == "D":
            pass_block(slot, half, to, P1 if to < STEP[slot] else OWN, (to - STEP[slot]) % COLS)
        else:
            back = 1 if route == "F" else -1
            pass_block(slot, half, to, AB1 if route == "F" else AB3, (to - back) % COLS)

    def far_block(slot, half, to, route):
        if route == "x":
            pass_block(slot, half, to, P2 if to < STEP[slot] else P1, (to - STEP[slot]) % COLS)
        elif route == "z":
            pass_block(slot, half, to, BEFORE[slot], to, True)
        else:
            back = 1 if route == "F" else -1
            pass_block(slot, half, to, BC1 if route == "F" else BC3, (to - back) % COLS)

    def two_back(half, to, route):
        if route == "F":
            ensure(P1, half, range(COLS))
            send(z == to - 1, P1, P2, half, 1, 0, 0)
        elif route == "D":
            send(z == to - 2, OWN, P2, half, 2, 0, 0)
        else:
            send(z == to - 2, OWN, RELAY, half, -1, 0, 0)

    def relayed(half):
        @pl.when(z == ROWS - 1)
        def _():
            kv_copy(OWN, RELAY, half, 0, 1).wait_recv()

        send(z == ROWS - 1, RELAY, P2, half, -1, 0, 0)

    mask = (cc <= rr) & (segrow == segcol)
    upper = jnp.where(rr <= cc, 1.0, 0.0)
    eyef = jnp.where(eye, 1.0, 0.0)
    keep = jnp.where(segrow == segrow[:, count - 1 : count], 1.0, 0.0)
    live = jnp.where(segrow == segrow[:, 0:1], 1.0, 0.0)
    h16 = lax.broadcasted_iota(jnp.int32, (2 * PER, GW), 0) % PER
    spread = jnp.where(h16 == lax.broadcasted_iota(jnp.int32, (2 * PER, GW), 1) // HEAD_P, 1.0, 0.0)
    spread_bf = spread.astype(bf16)
    hi = lax.Precision.HIGHEST
    low_half = lax.broadcasted_iota(jnp.int32, (count, 2 * HEAD_P), 1) < HEAD_P
    meta_rows = lax.broadcasted_iota(jnp.int32, (16, GW), 0)
    last_own, first_own = segrow[:, count - 1 : count], segrow[:, 0:1]

    def expand(value):
        top = value.astype(bf16)
        rest = (value - top.astype(f32)).astype(bf16)
        return dot(jnp.concatenate([top, rest], axis=0), spread_bf, 0, 0)

    head_rows = lax.broadcasted_iota(jnp.int32, (PER, 1), 0)

    def per_head(ref, g):
        out = jnp.zeros((PER, 1), f32)
        for j in range(PER):
            out = jnp.where(head_rows == j, ref[g * PER + j], out)
        return out

    grad_part[...] = jnp.zeros_like(grad_part)

    def pack(span, last, first):
        top = span.astype(bf16).astype(f32)
        middle = (span - top).astype(bf16).astype(f32)
        out = jnp.where(meta_rows == 0, top, jnp.where(meta_rows == 1, middle, span - top - middle))
        out = jnp.where(meta_rows == 3, last, jnp.where(meta_rows == 4, first, out))
        return out.astype(bf16)

    def unpack(block):
        m = block.astype(f32)
        return m[0:1] + m[1:2] + m[2:3], m[3:4], m[4:5]

    def mixer_group(g, _):
        cols = pl.ds(pl.multiple_of(g * GW, GW), GW)
        ncols = pl.ds(pl.multiple_of(g * STATE, STATE), STATE)
        steps = step_ref[pl.ds(pl.multiple_of(g * PER, PER), PER), :]
        cs = dot(steps, upper, 1, 0, hi) * (-jnp.exp(per_head(rate_ref, g)))
        skip_row = jnp.sum(spread[:PER] * per_head(skip_ref, g), axis=0, keepdims=True)
        cst = dot(eyef, cs, 1, 1, hi)
        span = cs[:, count - 1 : count]
        tail = span - cs
        e = jnp.exp(tail) * keep
        f = jnp.exp(cs) * live
        xg, gg = x_ref[:, cols], g_ref[:, cols]
        bg, cg = b_ref[:, ncols].astype(bf16), c_ref[:, ncols].astype(bf16)
        right = jnp.concatenate([(xg * expand(e)).astype(bf16), (xg * expand(e * tail)).astype(bf16)], axis=1)
        sh = dot(bg, right, 0, 0).astype(bf16)
        st_own[g % 2, g // 2, :STATE] = sh[:, :GW]
        st_own[g % 2, g // 2, STATE : 2 * STATE] = sh[:, GW:]
        fe = expand(f)
        fexp_ref[g] = fe
        right = jnp.concatenate([(gg * fe).astype(bf16), (gg * expand(f * cs)).astype(bf16)], axis=1)
        dd = dot(cg, right, 0, 0)
        d_ref[g] = dd[:, :GW]
        dh_ref[g] = dd[:, GW:]
        span_row = jnp.sum(spread[:PER] * span, axis=0, keepdims=True)
        st_own[g % 2, g // 2, 2 * STATE :] = pack(span_row, last_own, first_own)
        inner = dot(cg, bg, 1, 1)
        sums = []
        for pair in range(PER // 2):
            lanes = slice(pair * 2 * HEAD_P, (pair + 1) * 2 * HEAD_P)
            xp, gp = xg[:, lanes], gg[:, lanes]
            xpb, gpb = xp.astype(bf16), gp.astype(bf16)
            near = None
            for half in range(2):
                j = pair * 2 + half
                mine = low_half if half == 0 else jnp.logical_not(low_half)
                gap = jnp.where(mask, cst[:, j : j + 1] - cs[j : j + 1, :], FAR_BELOW)
                weight = jnp.exp(gap) * inner
                pairs = dot(jnp.where(mine, gpb, jnp.zeros_like(gpb)), xpb, 1, 1)
                sums.append(jnp.sum(weight * gap * pairs, axis=0, keepdims=True))
                part = dot(weight.astype(bf16), jnp.where(mine, xpb, jnp.zeros_like(xpb)), 1, 0)
                near = part if near is None else near + part
            at = pl.ds(pl.multiple_of(g * GW + pair * 2 * HEAD_P, 2 * HEAD_P), 2 * HEAD_P)
            near_ref[:, at] = near + xp * skip_row[:, lanes]
        sums = jnp.concatenate(sums, axis=0)
        rest = jnp.concatenate([sums[:, WIDTH:], jnp.zeros((PER, 2 * WIDTH - count), f32)], axis=1)
        grad_part[pl.ds(pl.multiple_of(g * PER, PER), PER), :] = sums[:, :WIDTH] + rest
        return 0

    def a_copy(c, d):
        return pltpu.make_async_remote_copy(
            src_ref=st_own.at[c, (x + d) % COLS], dst_ref=st_row.at[c, x],
            send_sem=a_ss.at[c, d - 1], recv_sem=a_rs.at[c, d - 1],
            device_id=dev(0, d), device_id_type=MESH,
        )

    def mixer_half(c):
        if c == 0:
            await_all(mixer_in)
        lax.fori_loop(0, GROUPS // 2, lambda k, u: mixer_group(2 * k + c, u), 0)
        for d in (2, 1, 3):
            a_copy(c, d).start()
        st_row[c, x] = st_own[c, x]

    scale = math.log2(math.e) / math.sqrt(WIDTH)

    def lanes_of(h, which):
        at = WIDTH + (2 * (h // (KV_HEADS // 2)) + which) * KEYS + (h % (KV_HEADS // 2)) * WIDTH
        return pl.ds(pl.multiple_of(at, WIDTH), WIDTH)

    def scores(slot, h):
        keys = kvb[slot, :, lanes_of(h, 0)]
        return dot(jnp.concatenate([keys, kvb[slot, :, :WIDTH]], axis=1), qs[h], 1, 1)

    def values_of(slot, h):
        return kvb[slot, :, lanes_of(h, 1)]

    def own_head(h, _):
        s = scores(OWN, h) + bias[...]
        top = jnp.max(s, axis=0, keepdims=True)
        w = jnp.exp2((s - top) * scale)
        mrow[pl.ds(h, 1), :] = top
        lrow[pl.ds(h, 1), :] = jnp.sum(w, axis=0, keepdims=True)
        acc[h] = dot(values_of(OWN, h), w.astype(bf16), 0, 0)
        return 0

    def heads_of(half):
        return half * KV_HEADS // 2, (half + 1) * KV_HEADS // 2

    causal = jnp.where(rr <= cc, 0.0, FAR_BELOW)
    bias[...] = jnp.concatenate([causal] * REP, axis=1)

    def attend_own(half):
        if half == 0:
            await_all(query_in)
        for h in range(*heads_of(half)):
            for r in range(REP):
                head = h * REP + r
                qs[h, r * count : (r + 1) * count, :WIDTH] = q_ref[:, head * WIDTH : (head + 1) * WIDTH]
                qs[h, r * count : (r + 1) * count, WIDTH:] = onehot
        lax.fori_loop(*heads_of(half), own_head, 0)

    def attend(slot, half):
        def head(h, _):
            s = scores(slot, h)
            before = mrow[pl.ds(h, 1), :]
            top = jnp.maximum(before, jnp.max(s, axis=0, keepdims=True))
            w = jnp.exp2((s - top) * scale)
            fade = jnp.exp2((before - top) * scale)
            mrow[pl.ds(h, 1), :] = top
            lrow[pl.ds(h, 1), :] = lrow[pl.ds(h, 1), :] * fade + jnp.sum(w, axis=0, keepdims=True)
            acc[h] = acc[h] * fade + dot(values_of(slot, h), w.astype(bf16), 0, 0)
            return 0

        lax.fori_loop(*heads_of(half), head, 0)

    def states(ref, *at):
        return ref[(*at, slice(0, STATE))].astype(f32), ref[(*at, slice(STATE, 2 * STATE))].astype(f32)

    def facts(ref, *at):
        return unpack(ref[(*at, slice(2 * STATE, ST))])

    def join(s, hat, last, ref, *at):
        span, after, _ = facts(ref, *at)
        s_b, hat_b = states(ref, *at)
        fade = jnp.where(last == after, jnp.exp(span), 0.0)
        return fade * s + s_b, fade * (hat + span * s) + hat_b, after

    def r_copy(c, dz):
        return pltpu.make_async_remote_copy(
            src_ref=r_out.at[c], dst_ref=r_in.at[c, dz - 1], send_sem=r_ss.at[c, dz - 1],
            recv_sem=r_rs.at[c, dz - 1], device_id=dev(dz, 0), device_id_type=MESH,
        )

    def row_total(c):
        for d in (2, 1, 3):
            a_copy(c, d).wait_recv()
        s, hat = states(st_row, c, 0)
        total, last, _ = facts(st_row, c, 0)
        for k in range(1, COLS):
            total = total + facts(st_row, c, k)[0]
            s, hat, last = join(s, hat, last, st_row, c, k)
        r_out[c, :STATE] = s.astype(bf16)
        r_out[c, STATE : 2 * STATE] = hat.astype(bf16)
        r_out[c, 2 * STATE :] = pack(total, last, last)
        for dz in (1, 2):
            @pl.when(z + dz < ROWS)
            def _(dz=dz):
                r_copy(c, dz).start()

            @pl.when(z - dz < 0)
            def _(dz=dz):
                r_in[c, dz - 1, : 2 * STATE] = jnp.zeros((2 * STATE, GW), bf16)
                r_in[c, dz - 1, 2 * STATE :] = jnp.full((16, GW), -1.0, bf16)

    def f_copy(c, d):
        return pltpu.make_async_remote_copy(
            src_ref=f_out.at[c, (x + d) % COLS], dst_ref=f_in.at[c, x],
            send_sem=f_ss.at[c, d - 1], recv_sem=f_rs.at[c, d - 1],
            device_id=dev(0, d), device_id_type=MESH,
        )

    def entering(c):
        for dz in (1, 2):
            @pl.when(z - dz >= 0)
            def _(dz=dz):
                r_copy(c, dz).wait_recv()
        s, hat = states(r_in, c, 1)
        s, hat, last = join(s, hat, facts(r_in, c, 1)[1], r_in, c, 0)
        for k in range(COLS):
            goes_on = jnp.where(facts(st_row, c, k)[2] == last, 1.0, 0.0)
            f_out[c, k, :STATE] = (s * goes_on).astype(bf16)
            f_out[c, k, STATE:] = (hat * goes_on).astype(bf16)
            if k < COLS - 1:
                s, hat, last = join(s, hat, last, st_row, c, k)
        for d in (2, 1, 3):
            f_copy(c, d).start()
        f_in[c, x] = f_out[c, x]

    def meet(slot, half):
        ensure(slot, 0, range(COLS))
        if half == 1:
            ensure(slot, 1, range(COLS))

        @pl.when(me >= BACK[slot])
        def _():
            attend(slot, half)

    def far_group(c, k):
        g = 2 * k + c
        cols = pl.ds(pl.multiple_of(g * GW, GW), GW)
        ncols = pl.ds(pl.multiple_of(g * STATE, STATE), STATE)
        s_in, hat_in = f_in[c, k, :STATE], f_in[c, k, STATE:]
        far = dot(c_ref[:, ncols].astype(bf16), s_in, 1, 0) * fexp_ref[g]
        mo_ref[:, cols] = (near_ref[:, cols] + far).astype(bf16)
        terms = hat_in.astype(f32) * d_ref[g] + s_in.astype(f32) * dh_ref[g]
        by_head = spread[:PER] * jnp.sum(terms, axis=0, keepdims=True)
        at = pl.ds(pl.multiple_of(g * PER, PER), PER)
        grad_part[at, :] = grad_part[at, :] + sum(by_head[:, i * WIDTH : (i + 1) * WIDTH] for i in range(GW // WIDTH))
        return 0

    def far_half(c):
        for d in (2, 1, 3):
            f_copy(c, d).wait_recv()
        lax.fori_loop(0, GROUPS // 2, lambda k, _: far_group(c, k), 0)

    def gc_copy(k):
        return pltpu.make_async_remote_copy(
            src_ref=g_own.at[0], dst_ref=g_ctx.at[me], send_sem=gc_ss.at[k],
            recv_sem=gc_rs.at[k], device_id={"ctx": (me + k) % n_ctx}, device_id_type=MESH,
        )

    def gd_copy(k):
        return pltpu.make_async_remote_copy(
            src_ref=g_own.at[1], dst_ref=g_dp.at[row], send_sem=gd_ss.at[k],
            recv_sem=gd_rs.at[k], device_id={"dp": (row + k) % n_dp}, device_id_type=MESH,
        )

    def each(first, last, act):
        def one(k, _):
            act(k)
            return 0

        lax.fori_loop(first, last, one, 0)

    def window_sum():
        g_own[0] = dot(jnp.ones((8, WIDTH), f32), grad_part[...], 1, 1, hi)
        g_ctx[me] = g_own[0]
        each(1, n_ctx, lambda k: gc_copy(k).start())

    def whole_sum():
        each(1, n_ctx, lambda k: gc_copy(k).wait_recv())
        g_own[1] = lax.fori_loop(0, n_ctx, lambda k, t: t + g_ctx[k], jnp.zeros((8, WIDTH), f32))
        g_dp[row] = g_own[1]
        each(1, n_dp, lambda k: gd_copy(k).start())

    def attention_out(half):
        lanes = pl.ds(half * REP * KEYS, REP * KEYS)
        return pltpu.make_async_copy(ao_ref.at[:, lanes], ao_hbm.at[:, lanes], out_sem.at[half])

    mixer_out = pltpu.make_async_copy(mo_ref, mo_hbm, out_sem.at[2])

    def finish(half):
        for h in range(*heads_of(half)):
            out = (acc[h] / lrow[h : h + 1, :]).T.astype(bf16)
            for r in range(REP):
                head = h * REP + r
                ao_ref[:, head * WIDTH : (head + 1) * WIDTH] = out[r * count : (r + 1) * count]
        attention_out(half).start()

    last = {step[0] + str(step[-1]) if step[0] == "ATT" else step[0]: i for i, step in enumerate(PLAN)}
    for i, (name, *what) in enumerate(PLAN):
        if name == "P1":
            send(z < ROWS - 1, OWN, P1, what[0], 1, 0, 0)
        elif name == "ATT" and what[0] == OWN:
            attend_own(what[1])
        elif name == "ATT":
            meet(*what)
        else:
            {"P2": two_back, "RL": relayed, "AB": near_block, "BC": far_block,
             "AB2": lambda half, to, route: near_block(AB2, half, to, route), "MIX": mixer_half, "RT": row_total, "ENT": entering, "FAR": far_half,
             "G1": window_sum, "G2": whole_sum}[name](*what)
        if name == "ATT" and last["ATT" + str(what[1])] == i:
            finish(what[1])
        if name == "FAR" and last["FAR"] == i:
            mixer_out.start()

    each(1, n_dp, lambda k: gd_copy(k).wait_recv())
    total = lax.fori_loop(0, n_dp, lambda k, t: t + g_dp[k], jnp.zeros((8, WIDTH), f32))
    dg_ref[...] = total * (1.0 / (n_ctx * n_dp * count))
    each(1, n_ctx, lambda k: gc_copy(k).wait_send())
    each(1, n_dp, lambda k: gd_copy(k).wait_send())

    await_all([mixer_out, attention_out(0), attention_out(1)])

    for when, copy in sent:
        @pl.when(when)
        def _(copy=copy):
            kv_copy(*copy).wait_send()

    for c in range(2):
        for d in (1, 2, 3):
            a_copy(c, d).wait_send()
            f_copy(c, d).wait_send()
        for dz in (1, 2):
            @pl.when(z + dz < ROWS)
            def _(c=c, dz=dz):
                r_copy(c, dz).wait_send()


def fused(q, k, v, seg, x, b, c, step, rate, skip, g):
    count = q.shape[0]
    vmem = pl.BlockSpec(memory_space=pltpu.VMEM)
    smem = pl.BlockSpec(memory_space=pltpu.SMEM)
    hbm = pl.BlockSpec(memory_space=pl.ANY)
    dma = pltpu.SemaphoreType.DMA
    n_ctx, n_dp = lax.axis_size("ctx"), lax.axis_size("dp")
    return pl.pallas_call(
        kernel,
        out_shape=(
            jax.ShapeDtypeStruct((count, Q_HEADS * WIDTH), bf16),
            jax.ShapeDtypeStruct((count, SSD_HEADS * HEAD_P), bf16),
            jax.ShapeDtypeStruct((8, WIDTH), f32),
        ),
        in_specs=[hbm] * 3 + [vmem] + [hbm] * 3 + [vmem] + [smem] * 2 + [hbm],
        out_specs=(hbm, hbm, vmem),
        scratch_shapes=[
            pltpu.VMEM((count, Q_HEADS * WIDTH), bf16),
            pltpu.VMEM((count, SSD_HEADS * HEAD_P), bf16),
            pltpu.VMEM((count, Q_HEADS * WIDTH), bf16),
            pltpu.VMEM((count, SSD_HEADS * HEAD_P), f32),
            pltpu.VMEM((count, GROUPS * STATE), f32),
            pltpu.VMEM((count, GROUPS * STATE), f32),
            pltpu.VMEM((count, SSD_HEADS * HEAD_P), f32),
            dma((9,)),
            dma((3,)),
            pltpu.VMEM((10, count, KVW), bf16),
            pltpu.VMEM((KV_HEADS, REP * count, 2 * WIDTH), bf16),
            pltpu.VMEM((KV_HEADS, WIDTH, REP * count), f32),
            pltpu.VMEM((KV_HEADS, REP * count), f32),
            pltpu.VMEM((KV_HEADS, REP * count), f32),
            pltpu.VMEM((count, REP * count), f32),
            pltpu.VMEM((2, COLS, ST, GW), bf16),
            pltpu.VMEM((2, COLS, ST, GW), bf16),
            pltpu.VMEM((2, ST, GW), bf16),
            pltpu.VMEM((2, 2, ST, GW), bf16),
            pltpu.VMEM((2, COLS, 2 * STATE, GW), bf16),
            pltpu.VMEM((2, COLS, 2 * STATE, GW), bf16),
            pltpu.VMEM((GROUPS, STATE, GW), f32),
            pltpu.VMEM((GROUPS, STATE, GW), f32),
            pltpu.VMEM((GROUPS, count, GW), f32),
            pltpu.VMEM((count, SSD_HEADS * HEAD_P), f32),
            pltpu.VMEM((WIDTH, WIDTH), f32),
            pltpu.VMEM((2, 8, WIDTH), f32),
            pltpu.VMEM((n_ctx, 8, WIDTH), f32),
            pltpu.VMEM((n_dp, 8, WIDTH), f32),
            dma((10, 2, 4)), dma((10, 2)),
            dma((2, 3)), dma((2, 3)), dma((2, 2)), dma((2, 2)), dma((2, 3)), dma((2, 3)),
            dma((n_ctx,)), dma((n_ctx,)), dma((n_dp,)), dma((n_dp,)),
        ],
        compiler_params=pltpu.CompilerParams(
            collective_id=0, has_side_effects=True, vmem_limit_bytes=60 * 2**20
        ),
        name="fused_mixer_attention",
    )(q, k, v, seg, x, b, c, step, rate, skip, g)


def hand_over_kernel(a_in, m_in, g_in, a_out, m_out, g_out, held, in_sem, out_sem):
    rows = a_in.shape[0] // PIECES
    pieces = [(j, i, pl.ds(i * rows, rows)) for i in range(PIECES) for j in range(2)]
    come = [
        pltpu.make_async_copy((a_in, m_in)[j].at[at], held.at[j, at], in_sem.at[j, i])
        for j, i, at in pieces
    ]
    leave = [
        pltpu.make_async_copy(held.at[j, at], (a_out, m_out)[j].at[at], out_sem.at[j, i])
        for j, i, at in pieces
    ]
    for copy in come:
        copy.start()
    g_out[...] = g_in[0, :SSD_HEADS]
    for copy, following in zip(come, leave):
        copy.wait()
        following.start()
    for copy in leave:
        copy.wait()


def hand_over(a, m, g):
    hbm, vmem = pl.BlockSpec(memory_space=pl.ANY), pl.BlockSpec(memory_space=pltpu.VMEM)
    return pl.pallas_call(
        hand_over_kernel,
        out_shape=(
            jax.ShapeDtypeStruct(a.shape, a.dtype),
            jax.ShapeDtypeStruct(m.shape, m.dtype),
            jax.ShapeDtypeStruct((SSD_HEADS,), f32),
        ),
        in_specs=[hbm, hbm, vmem],
        out_specs=(hbm, hbm, vmem),
        scratch_shapes=[
            pltpu.VMEM((2, *a.shape), a.dtype),
            pltpu.SemaphoreType.DMA((2, PIECES)),
            pltpu.SemaphoreType.DMA((2, PIECES)),
        ],
        name="hand_over",
    )(a, m, g)


def on_device(
    queries, keys, values, segment_ids, ssd_input, b_matrix, c_matrix, step_size,
    decay_log, skip_gain, cotangent,
):
    attention, mixed, decay_grad = fused(
        queries[0], keys[0], values[0], segment_ids, ssd_input[0], b_matrix[0], c_matrix[0],
        step_size[0], decay_log, skip_gain, cotangent[0],
    )
    attention, mixed, decay_grad = hand_over(attention, mixed, decay_grad)
    return attention[None], mixed[None], decay_grad


def solution(mesh):
    tok = P("dp", "ctx", None)
    return jax.shard_map(
        on_device,
        mesh=mesh,
        in_specs=(tok, tok, tok, P("dp", "ctx"), tok, tok, tok, P("dp", None, "ctx"), P(), P(), tok),
        out_specs=(tok, tok, P()),
        check_vma=False,
    )
```

```python
import functools
import functools
import math

import jax
import jax.numpy as jnp
from jax import lax
from jax.experimental import pallas as pl
from jax.experimental.pallas import tpu as pltpu
from jax.sharding import PartitionSpec as P

Q_HEADS = 32
KV_HEADS = 8
REP = Q_HEADS // KV_HEADS
WIDTH = 128
SSD_HEADS = 64
HEAD_P = 64
STATE = 128
GROUPS = 8
PER = SSD_HEADS // GROUPS
GW = PER * HEAD_P
COLS = 4
ROWS = 4
KVW = 2 * KV_HEADS * WIDTH + WIDTH
FAR_BELOW = -1e30
MESH = pl.DeviceIdType.MESH

OWN, P1, P2, AB1, AB3, AB2, BC1, BC3, BC2, RELAY = range(10)
BACK = (0, 4, 8, 1, 3, 2, 5, 7, 6)
STEP = {AB1: 1, AB2: 2, AB3: 3, BC1: 1, BC2: 2, BC3: 3}
BEFORE = {BC1: AB1, BC2: AB2, BC3: AB3}
PLAN = (
    ("P2", 0, 3, "D"), ("AB", AB1, 1, 2), ("AB", AB1, 0, 1), ("AB2", 0, 3, "D"), ("P1", 1),
    ("AB", AB1, 0, 3), ("P1", 0), ("MIX", 0), ("P2", 1, 3, "D"), ("MIX", 1), ("P2", 1, 2, "F"),
    ("ATT", OWN, 0), ("P2", 0, 2, "R"), ("AB", AB1, 0, 0), ("BC", BC1, 0, 1, "z"), ("ATT", P1, 0),
    ("BC", BC1, 1, 2, "z"), ("AB", AB3, 0, 3), ("BC", BC1, 0, 3, "z"), ("AB", AB3, 1, 0),
    ("AB", AB1, 0, 2), ("ATT", OWN, 1), ("AB", AB3, 1, 3), ("AB", AB1, 1, 1), ("AB", AB3, 0, 2),
    ("AB", AB3, 0, 1), ("AB", AB3, 0, 0), ("AB", AB3, 1, 2), ("AB2", 1, 3, "F"), ("AB", AB1, 1, 3),
    ("RT", 0), ("RL", 0), ("AB2", 0, 2, "F"), ("RT", 1), ("AB2", 0, 0, "M"), ("AB", AB1, 1, 0),
    ("BC", BC1, 1, 1, "x"), ("BC", BC1, 1, 3, "x"), ("AB", AB3, 1, 1), ("ATT", P1, 1), ("ATT", P2, 1),
    ("AB2", 1, 1, "M"), ("BC", BC3, 0, 2, "x"), ("BC", BC3, 0, 3, "x"), ("AB2", 1, 2, "F"),
    ("BC", BC1, 0, 0, "z"), ("AB2", 0, 1, "F"), ("BC", BC1, 1, 0, "x"), ("ATT", AB3, 1),
    ("BC", BC3, 1, 3, "z"), ("BC", BC2, 1, 3, "z"), ("ENT", 0), ("ATT", AB1, 0), ("BC", BC3, 0, 0, "z"),
    ("BC", BC1, 0, 2, "z"), ("BC", BC3, 0, 1, "z"), ("ATT", AB3, 0), ("ATT", AB1, 1),
    ("BC", BC3, 1, 1, "z"), ("ENT", 1), ("BC", BC3, 1, 0, "z"), ("ATT", BC1, 1), ("BC", BC2, 0, 1, "M"),
    ("BC", BC3, 1, 2, "z"), ("AB2", 1, 0, "M"), ("ATT", BC1, 0), ("ATT", AB2, 0), ("ATT", P2, 0),
    ("BC", BC2, 1, 1, "F"), ("BC", BC2, 0, 3, "z"), ("FAR", 0), ("BC", BC2, 1, 0, "x"),
    ("BC", BC2, 1, 2, "F"), ("BC", BC2, 0, 2, "z"), ("BC", BC2, 0, 0, "z"), ("ATT", BC3, 0),
    ("ATT", BC3, 1), ("FAR", 1), ("G1",), ("ATT", AB2, 1), ("G2",), ("ATT", BC2, 0), ("ATT", BC2, 1),
)
KEYS = KV_HEADS * WIDTH // 2
HALVES = ((0, WIDTH + 2 * KEYS), (WIDTH + 2 * KEYS, 2 * KEYS))
ST = 2 * STATE + 16
PIECES = 6

f32, bf16 = jnp.float32, jnp.bfloat16


def dot(a, b, ca, cb, precision=None):
    return lax.dot_general(
        a, b, (((ca,), (cb,)), ((), ())), precision=precision, preferred_element_type=f32
    )


def kernel(
    q_hbm, k_hbm, v_hbm, seg_ref, x_hbm, b_hbm, c_hbm, step_ref, rate_ref, skip_ref, g_hbm,
    ao_hbm, mo_hbm, dg_ref, ao_ref, mo_ref, q_ref, x_ref, b_ref, c_ref, g_ref, in_sem, out_sem,
    kvb, qs, acc, mrow, lrow, bias, st_own, st_row, r_out, r_in, f_out, f_in,
    d_ref, dh_ref, fexp_ref, near_ref, grad_part, g_own, g_ctx, g_dp,
    kv_ss, kv_rs, a_ss, a_rs, r_ss, r_rs, f_ss, f_rs, gc_ss, gc_rs, gd_ss, gd_rs,
):
    count = q_ref.shape[0]
    me = lax.axis_index("ctx")
    z, x = me // COLS, me % COLS

    def dev(dz, dx):
        return {"ctx": ((z + dz) % ROWS) * COLS + (x + dx) % COLS}

    def come_in(*pairs, first):
        return [
            pltpu.make_async_copy(src, to, in_sem.at[first + i]) for i, (src, to) in enumerate(pairs)
        ]

    def await_all(copies):
        for copy in copies:
            copy.wait()

    kv_in = come_in(
        *(
            (src.at[:, pl.ds(half * KEYS, KEYS)], kvb.at[OWN, :, pl.ds(WIDTH + (2 * half + i) * KEYS, KEYS)])
            for half in (0, 1) for i, src in enumerate((k_hbm, v_hbm))
        ), first=0,
    )
    mixer_in = come_in((b_hbm, b_ref), (c_hbm, c_ref), (x_hbm, x_ref), (g_hbm, g_ref), first=4)
    query_in = come_in((q_hbm, q_ref), first=8)
    for copy in kv_in + mixer_in + query_in:
        copy.start()

    n_ctx, n_dp = lax.axis_size("ctx"), lax.axis_size("dp")
    row = lax.axis_index("dp")
    barrier = pltpu.get_barrier_semaphore()

    def greet(axis, place, size):
        def one(k, _):
            to = {axis: (place + k) % size}
            pl.semaphore_signal(barrier, inc=1, device_id=to, device_id_type=MESH)
            return 0

        lax.fori_loop(1, size, one, 0)

    greet("ctx", me, n_ctx)
    greet("dp", row, n_dp)

    segrow = seg_ref[...].astype(f32)
    rr = lax.broadcasted_iota(jnp.int32, (count, count), 0)
    cc = lax.broadcasted_iota(jnp.int32, (count, count), 1)
    eye = rr == cc
    segcol = jnp.sum(jnp.where(eye, segrow, 0.0), axis=1, keepdims=True)
    lane = lax.broadcasted_iota(jnp.int32, (count, WIDTH), 1).astype(f32)
    onehot = jnp.where(lane == segcol, 1.0, 0.0).astype(bf16)
    other = jnp.where((lane != segcol) & (lane < 8.0), FAR_BELOW, 0.0).astype(bf16)
    kvb[OWN, :, :WIDTH] = other

    pl.semaphore_wait(barrier, n_ctx + n_dp - 2)
    await_all(kv_in)

    def kv_copy(src, slot, half, dz, dx, way=0):
        lanes = pl.ds(*HALVES[half])
        return pltpu.make_async_remote_copy(
            src_ref=kvb.at[src, :, lanes], dst_ref=kvb.at[slot, :, lanes],
            send_sem=kv_ss.at[slot, half, way], recv_sem=kv_rs.at[slot, half],
            device_id=dev(dz, dx), device_id_type=MESH,
        )

    sent, here, ways = [], set(), {}

    def send(when, source, slot, half, dz, dx, where):
        way = ways.get((slot, half, where), 0)
        ways[slot, half, where] = way + 1
        copy = (source, slot, half, dz, dx, way)

        @pl.when(when)
        def _():
            kv_copy(*copy).start()

        sent.append((when, copy))

    def ensure(slot, half, columns):
        todo = [k for k in columns if (slot, half, k) not in here]
        here.update((slot, half, k) for k in todo)
        if todo:
            when = me >= BACK[slot]
            if len(todo) < COLS:
                when = when & functools.reduce(jnp.logical_or, [x == k for k in todo])

            @pl.when(when)
            def _():
                kv_copy(OWN, slot, half, 0, 1).wait_recv()

    def pass_block(slot, half, to, source, start, by_z=False):
        first = -(-(BACK[slot] - to) // COLS)
        if source != OWN:
            ensure(source, half, (start,))
        if by_z:
            send((x == start) & (z >= first - 1) & (z < ROWS - 1), source, slot, half, 1, 0, start)
        else:
            send((x == start) & (z >= first), source, slot, half, 0, (to - start) % COLS, start)

    def near_block(slot, half, to, route="D"):
        if route == "D":
            pass_block(slot, half, to, P1 if to < STEP[slot] else OWN, (to - STEP[slot]) % COLS)
        else:
            back = 1 if route == "F" else -1
            pass_block(slot, half, to, AB1 if route == "F" else AB3, (to - back) % COLS)

    def far_block(slot, half, to, route):
        if route == "x":
            pass_block(slot, half, to, P2 if to < STEP[slot] else P1, (to - STEP[slot]) % COLS)
        elif route == "z":
            pass_block(slot, half, to, BEFORE[slot], to, True)
        else:
            back = 1 if route == "F" else -1
            pass_block(slot, half, to, BC1 if route == "F" else BC3, (to - back) % COLS)

    def two_back(half, to, route):
        if route == "F":
            ensure(P1, half, range(COLS))
            send(z == to - 1, P1, P2, half, 1, 0, 0)
        elif route == "D":
            send(z == to - 2, OWN, P2, half, 2, 0, 0)
        else:
            send(z == to - 2, OWN, RELAY, half, -1, 0, 0)

    def relayed(half):
        @pl.when(z == ROWS - 1)
        def _():
            kv_copy(OWN, RELAY, half, 0, 1).wait_recv()

        send(z == ROWS - 1, RELAY, P2, half, -1, 0, 0)

    mask = (cc <= rr) & (segrow == segcol)
    upper = jnp.where(rr <= cc, 1.0, 0.0)
    eyef = jnp.where(eye, 1.0, 0.0)
    keep = jnp.where(segrow == segrow[:, count - 1 : count], 1.0, 0.0)
    live = jnp.where(segrow == segrow[:, 0:1], 1.0, 0.0)
    h16 = lax.broadcasted_iota(jnp.int32, (2 * PER, GW), 0) % PER
    spread = jnp.where(h16 == lax.broadcasted_iota(jnp.int32, (2 * PER, GW), 1) // HEAD_P, 1.0, 0.0)
    spread_bf = spread.astype(bf16)
    hi = lax.Precision.HIGHEST
    low_half = lax.broadcasted_iota(jnp.int32, (count, 2 * HEAD_P), 1) < HEAD_P
    meta_rows = lax.broadcasted_iota(jnp.int32, (16, GW), 0)
    last_own, first_own = segrow[:, count - 1 : count], segrow[:, 0:1]

    def expand(value):
        top = value.astype(bf16)
        rest = (value - top.astype(f32)).astype(bf16)
        return dot(jnp.concatenate([top, rest], axis=0), spread_bf, 0, 0)

    head_rows = lax.broadcasted_iota(jnp.int32, (PER, 1), 0)

    def per_head(ref, g):
        out = jnp.zeros((PER, 1), f32)
        for j in range(PER):
            out = jnp.where(head_rows == j, ref[g * PER + j], out)
        return out

    grad_part[...] = jnp.zeros_like(grad_part)

    def pack(span, last, first):
        top = span.astype(bf16).astype(f32)
        middle = (span - top).astype(bf16).astype(f32)
        out = jnp.where(meta_rows == 0, top, jnp.where(meta_rows == 1, middle, span - top - middle))
        out = jnp.where(meta_rows == 3, last, jnp.where(meta_rows == 4, first, out))
        return out.astype(bf16)

    def unpack(block):
        m = block.astype(f32)
        return m[0:1] + m[1:2] + m[2:3], m[3:4], m[4:5]

    def mixer_group(g, _):
        cols = pl.ds(pl.multiple_of(g * GW, GW), GW)
        ncols = pl.ds(pl.multiple_of(g * STATE, STATE), STATE)
        steps = step_ref[pl.ds(pl.multiple_of(g * PER, PER), PER), :]
        cs = dot(steps, upper, 1, 0, hi) * (-jnp.exp(per_head(rate_ref, g)))
        skip_row = jnp.sum(spread[:PER] * per_head(skip_ref, g), axis=0, keepdims=True)
        cst = dot(eyef, cs, 1, 1, hi)
        span = cs[:, count - 1 : count]
        tail = span - cs
        e = jnp.exp(tail) * keep
        f = jnp.exp(cs) * live
        xg, gg = x_ref[:, cols], g_ref[:, cols]
        bg, cg = b_ref[:, ncols].astype(bf16), c_ref[:, ncols].astype(bf16)
        right = jnp.concatenate([(xg * expand(e)).astype(bf16), (xg * expand(e * tail)).astype(bf16)], axis=1)
        sh = dot(bg, right, 0, 0).astype(bf16)
        st_own[g % 2, g // 2, :STATE] = sh[:, :GW]
        st_own[g % 2, g // 2, STATE : 2 * STATE] = sh[:, GW:]
        fe = expand(f)
        fexp_ref[g] = fe
        right = jnp.concatenate([(gg * fe).astype(bf16), (gg * expand(f * cs)).astype(bf16)], axis=1)
        dd = dot(cg, right, 0, 0)
        d_ref[g] = dd[:, :GW]
        dh_ref[g] = dd[:, GW:]
        span_row = jnp.sum(spread[:PER] * span, axis=0, keepdims=True)
        st_own[g % 2, g // 2, 2 * STATE :] = pack(span_row, last_own, first_own)
        inner = dot(cg, bg, 1, 1)
        sums = []
        for pair in range(PER // 2):
            lanes = slice(pair * 2 * HEAD_P, (pair + 1) * 2 * HEAD_P)
            xp, gp = xg[:, lanes], gg[:, lanes]
            xpb, gpb = xp.astype(bf16), gp.astype(bf16)
            near = None
            for half in range(2):
                j = pair * 2 + half
                mine = low_half if half == 0 else jnp.logical_not(low_half)
                gap = jnp.where(mask, cst[:, j : j + 1] - cs[j : j + 1, :], FAR_BELOW)
                weight = jnp.exp(gap) * inner
                pairs = dot(jnp.where(mine, gpb, jnp.zeros_like(gpb)), xpb, 1, 1)
                sums.append(jnp.sum(weight * gap * pairs, axis=0, keepdims=True))
                part = dot(weight.astype(bf16), jnp.where(mine, xpb, jnp.zeros_like(xpb)), 1, 0)
                near = part if near is None else near + part
            at = pl.ds(pl.multiple_of(g * GW + pair * 2 * HEAD_P, 2 * HEAD_P), 2 * HEAD_P)
            near_ref[:, at] = near + xp * skip_row[:, lanes]
        sums = jnp.concatenate(sums, axis=0)
        rest = jnp.concatenate([sums[:, WIDTH:], jnp.zeros((PER, 2 * WIDTH - count), f32)], axis=1)
        grad_part[pl.ds(pl.multiple_of(g * PER, PER), PER), :] = sums[:, :WIDTH] + rest
        return 0

    def a_copy(c, d):
        return pltpu.make_async_remote_copy(
            src_ref=st_own.at[c, (x + d) % COLS], dst_ref=st_row.at[c, x],
            send_sem=a_ss.at[c, d - 1], recv_sem=a_rs.at[c, d - 1],
            device_id=dev(0, d), device_id_type=MESH,
        )

    def mixer_half(c):
        if c == 0:
            await_all(mixer_in)
        lax.fori_loop(0, GROUPS // 2, lambda k, u: mixer_group(2 * k + c, u), 0)
        for d in (2, 1, 3):
            a_copy(c, d).start()
        st_row[c, x] = st_own[c, x]

    scale = math.log2(math.e) / math.sqrt(WIDTH)

    def lanes_of(h, which):
        at = WIDTH + (2 * (h // (KV_HEADS // 2)) + which) * KEYS + (h % (KV_HEADS // 2)) * WIDTH
        return pl.ds(pl.multiple_of(at, WIDTH), WIDTH)

    def scores(slot, h):
        keys = kvb[slot, :, lanes_of(h, 0)]
        return dot(jnp.concatenate([keys, kvb[slot, :, :WIDTH]], axis=1), qs[h], 1, 1)

    def values_of(slot, h):
        return kvb[slot, :, lanes_of(h, 1)]

    def own_head(h, _):
        s = scores(OWN, h) + bias[...]
        top = jnp.max(s, axis=0, keepdims=True)
        w = jnp.exp2((s - top) * scale)
        mrow[pl.ds(h, 1), :] = top
        lrow[pl.ds(h, 1), :] = jnp.sum(w, axis=0, keepdims=True)
        acc[h] = dot(values_of(OWN, h), w.astype(bf16), 0, 0)
        return 0

    def heads_of(half):
        return half * KV_HEADS // 2, (half + 1) * KV_HEADS // 2

    causal = jnp.where(rr <= cc, 0.0, FAR_BELOW)
    bias[...] = jnp.concatenate([causal] * REP, axis=1)

    def attend_own(half):
        if half == 0:
            await_all(query_in)
        for h in range(*heads_of(half)):
            for r in range(REP):
                head = h * REP + r
                qs[h, r * count : (r + 1) * count, :WIDTH] = q_ref[:, head * WIDTH : (head + 1) * WIDTH]
                qs[h, r * count : (r + 1) * count, WIDTH:] = onehot
        lax.fori_loop(*heads_of(half), own_head, 0, unroll=2)

    def attend(slot, half):
        def head(h, _):
            s = scores(slot, h)
            before = mrow[pl.ds(h, 1), :]
            top = jnp.maximum(before, jnp.max(s, axis=0, keepdims=True))
            w = jnp.exp2((s - top) * scale)
            fade = jnp.exp2((before - top) * scale)
            mrow[pl.ds(h, 1), :] = top
            lrow[pl.ds(h, 1), :] = lrow[pl.ds(h, 1), :] * fade + jnp.sum(w, axis=0, keepdims=True)
            acc[h] = acc[h] * fade + dot(values_of(slot, h), w.astype(bf16), 0, 0)
            return 0

        lax.fori_loop(*heads_of(half), head, 0, unroll=2)

    def states(ref, *at):
        return ref[(*at, slice(0, STATE))].astype(f32), ref[(*at, slice(STATE, 2 * STATE))].astype(f32)

    def facts(ref, *at):
        return unpack(ref[(*at, slice(2 * STATE, ST))])

    def join(s, hat, last, ref, *at):
        span, after, _ = facts(ref, *at)
        s_b, hat_b = states(ref, *at)
        fade = jnp.where(last == after, jnp.exp(span), 0.0)
        return fade * s + s_b, fade * (hat + span * s) + hat_b, after

    def r_copy(c, dz):
        return pltpu.make_async_remote_copy(
            src_ref=r_out.at[c], dst_ref=r_in.at[c, dz - 1], send_sem=r_ss.at[c, dz - 1],
            recv_sem=r_rs.at[c, dz - 1], device_id=dev(dz, 0), device_id_type=MESH,
        )

    def row_total(c):
        for d in (2, 1, 3):
            a_copy(c, d).wait_recv()
        s, hat = states(st_row, c, 0)
        total, last, _ = facts(st_row, c, 0)
        for k in range(1, COLS):
            total = total + facts(st_row, c, k)[0]
            s, hat, last = join(s, hat, last, st_row, c, k)
        r_out[c, :STATE] = s.astype(bf16)
        r_out[c, STATE : 2 * STATE] = hat.astype(bf16)
        r_out[c, 2 * STATE :] = pack(total, last, last)
        for dz in (1, 2):
            @pl.when(z + dz < ROWS)
            def _(dz=dz):
                r_copy(c, dz).start()

            @pl.when(z - dz < 0)
            def _(dz=dz):
                r_in[c, dz - 1, : 2 * STATE] = jnp.zeros((2 * STATE, GW), bf16)
                r_in[c, dz - 1, 2 * STATE :] = jnp.full((16, GW), -1.0, bf16)

    def f_copy(c, d):
        return pltpu.make_async_remote_copy(
            src_ref=f_out.at[c, (x + d) % COLS], dst_ref=f_in.at[c, x],
            send_sem=f_ss.at[c, d - 1], recv_sem=f_rs.at[c, d - 1],
            device_id=dev(0, d), device_id_type=MESH,
        )

    def entering(c):
        for dz in (1, 2):
            @pl.when(z - dz >= 0)
            def _(dz=dz):
                r_copy(c, dz).wait_recv()
        s, hat = states(r_in, c, 1)
        s, hat, last = join(s, hat, facts(r_in, c, 1)[1], r_in, c, 0)
        for k in range(COLS):
            goes_on = jnp.where(facts(st_row, c, k)[2] == last, 1.0, 0.0)
            f_out[c, k, :STATE] = (s * goes_on).astype(bf16)
            f_out[c, k, STATE:] = (hat * goes_on).astype(bf16)
            if k < COLS - 1:
                s, hat, last = join(s, hat, last, st_row, c, k)
        for d in (2, 1, 3):
            f_copy(c, d).start()
        f_in[c, x] = f_out[c, x]

    def meet(slot, half):
        ensure(slot, 0, range(COLS))
        if half == 1:
            ensure(slot, 1, range(COLS))

        @pl.when(me >= BACK[slot])
        def _():
            attend(slot, half)

    def far_group(c, k):
        g = 2 * k + c
        cols = pl.ds(pl.multiple_of(g * GW, GW), GW)
        ncols = pl.ds(pl.multiple_of(g * STATE, STATE), STATE)
        s_in, hat_in = f_in[c, k, :STATE], f_in[c, k, STATE:]
        far = dot(c_ref[:, ncols].astype(bf16), s_in, 1, 0) * fexp_ref[g]
        mo_ref[:, cols] = (near_ref[:, cols] + far).astype(bf16)
        terms = hat_in.astype(f32) * d_ref[g] + s_in.astype(f32) * dh_ref[g]
        by_head = spread[:PER] * jnp.sum(terms, axis=0, keepdims=True)
        at = pl.ds(pl.multiple_of(g * PER, PER), PER)
        grad_part[at, :] = grad_part[at, :] + sum(by_head[:, i * WIDTH : (i + 1) * WIDTH] for i in range(GW // WIDTH))
        return 0

    def far_half(c):
        for d in (2, 1, 3):
            f_copy(c, d).wait_recv()
        lax.fori_loop(0, GROUPS // 2, lambda k, _: far_group(c, k), 0)

    def gc_copy(k):
        return pltpu.make_async_remote_copy(
            src_ref=g_own.at[0], dst_ref=g_ctx.at[me], send_sem=gc_ss.at[k],
            recv_sem=gc_rs.at[k], device_id={"ctx": (me + k) % n_ctx}, device_id_type=MESH,
        )

    def gd_copy(k):
        return pltpu.make_async_remote_copy(
            src_ref=g_own.at[1], dst_ref=g_dp.at[row], send_sem=gd_ss.at[k],
            recv_sem=gd_rs.at[k], device_id={"dp": (row + k) % n_dp}, device_id_type=MESH,
        )

    def each(first, last, act):
        def one(k, _):
            act(k)
            return 0

        lax.fori_loop(first, last, one, 0)

    def window_sum():
        g_own[0] = dot(jnp.ones((8, WIDTH), f32), grad_part[...], 1, 1, hi)
        g_ctx[me] = g_own[0]
        each(1, n_ctx, lambda k: gc_copy(k).start())

    def whole_sum():
        each(1, n_ctx, lambda k: gc_copy(k).wait_recv())
        g_own[1] = lax.fori_loop(0, n_ctx, lambda k, t: t + g_ctx[k], jnp.zeros((8, WIDTH), f32))
        g_dp[row] = g_own[1]
        each(1, n_dp, lambda k: gd_copy(k).start())

    def attention_out(half):
        lanes = pl.ds(half * REP * KEYS, REP * KEYS)
        return pltpu.make_async_copy(ao_ref.at[:, lanes], ao_hbm.at[:, lanes], out_sem.at[half])

    mixer_out = pltpu.make_async_copy(mo_ref, mo_hbm, out_sem.at[2])

    def finish(half):
        for h in range(*heads_of(half)):
            out = (acc[h] / lrow[h : h + 1, :]).T.astype(bf16)
            for r in range(REP):
                head = h * REP + r
                ao_ref[:, head * WIDTH : (head + 1) * WIDTH] = out[r * count : (r + 1) * count]
        attention_out(half).start()

    last = {step[0] + str(step[-1]) if step[0] == "ATT" else step[0]: i for i, step in enumerate(PLAN)}
    for i, (name, *what) in enumerate(PLAN):
        if name == "P1":
            send(z < ROWS - 1, OWN, P1, what[0], 1, 0, 0)
        elif name == "ATT" and what[0] == OWN:
            attend_own(what[1])
        elif name == "ATT":
            meet(*what)
        else:
            {"P2": two_back, "RL": relayed, "AB": near_block, "BC": far_block,
             "AB2": lambda half, to, route: near_block(AB2, half, to, route), "MIX": mixer_half, "RT": row_total, "ENT": entering, "FAR": far_half,
             "G1": window_sum, "G2": whole_sum}[name](*what)
        if name == "ATT" and last["ATT" + str(what[1])] == i:
            finish(what[1])
        if name == "FAR" and last["FAR"] == i:
            mixer_out.start()

    each(1, n_dp, lambda k: gd_copy(k).wait_recv())
    total = lax.fori_loop(0, n_dp, lambda k, t: t + g_dp[k], jnp.zeros((8, WIDTH), f32))
    dg_ref[...] = total * (1.0 / (n_ctx * n_dp * count))
    each(1, n_ctx, lambda k: gc_copy(k).wait_send())
    each(1, n_dp, lambda k: gd_copy(k).wait_send())

    await_all([mixer_out, attention_out(0), attention_out(1)])

    for when, copy in sent:
        @pl.when(when)
        def _(copy=copy):
            kv_copy(*copy).wait_send()

    for c in range(2):
        for d in (1, 2, 3):
            a_copy(c, d).wait_send()
            f_copy(c, d).wait_send()
        for dz in (1, 2):
            @pl.when(z + dz < ROWS)
            def _(c=c, dz=dz):
                r_copy(c, dz).wait_send()


def fused(q, k, v, seg, x, b, c, step, rate, skip, g):
    count = q.shape[0]
    vmem = pl.BlockSpec(memory_space=pltpu.VMEM)
    smem = pl.BlockSpec(memory_space=pltpu.SMEM)
    hbm = pl.BlockSpec(memory_space=pl.ANY)
    dma = pltpu.SemaphoreType.DMA
    n_ctx, n_dp = lax.axis_size("ctx"), lax.axis_size("dp")
    return pl.pallas_call(
        kernel,
        out_shape=(
            jax.ShapeDtypeStruct((count, Q_HEADS * WIDTH), bf16),
            jax.ShapeDtypeStruct((count, SSD_HEADS * HEAD_P), bf16),
            jax.ShapeDtypeStruct((8, WIDTH), f32),
        ),
        in_specs=[hbm] * 3 + [vmem] + [hbm] * 3 + [vmem] + [smem] * 2 + [hbm],
        out_specs=(hbm, hbm, vmem),
        scratch_shapes=[
            pltpu.VMEM((count, Q_HEADS * WIDTH), bf16),
            pltpu.VMEM((count, SSD_HEADS * HEAD_P), bf16),
            pltpu.VMEM((count, Q_HEADS * WIDTH), bf16),
            pltpu.VMEM((count, SSD_HEADS * HEAD_P), f32),
            pltpu.VMEM((count, GROUPS * STATE), f32),
            pltpu.VMEM((count, GROUPS * STATE), f32),
            pltpu.VMEM((count, SSD_HEADS * HEAD_P), f32),
            dma((9,)),
            dma((3,)),
            pltpu.VMEM((10, count, KVW), bf16),
            pltpu.VMEM((KV_HEADS, REP * count, 2 * WIDTH), bf16),
            pltpu.VMEM((KV_HEADS, WIDTH, REP * count), f32),
            pltpu.VMEM((KV_HEADS, REP * count), f32),
            pltpu.VMEM((KV_HEADS, REP * count), f32),
            pltpu.VMEM((count, REP * count), f32),
            pltpu.VMEM((2, COLS, ST, GW), bf16),
            pltpu.VMEM((2, COLS, ST, GW), bf16),
            pltpu.VMEM((2, ST, GW), bf16),
            pltpu.VMEM((2, 2, ST, GW), bf16),
            pltpu.VMEM((2, COLS, 2 * STATE, GW), bf16),
            pltpu.VMEM((2, COLS, 2 * STATE, GW), bf16),
            pltpu.VMEM((GROUPS, STATE, GW), f32),
            pltpu.VMEM((GROUPS, STATE, GW), f32),
            pltpu.VMEM((GROUPS, count, GW), f32),
            pltpu.VMEM((count, SSD_HEADS * HEAD_P), f32),
            pltpu.VMEM((WIDTH, WIDTH), f32),
            pltpu.VMEM((2, 8, WIDTH), f32),
            pltpu.VMEM((n_ctx, 8, WIDTH), f32),
            pltpu.VMEM((n_dp, 8, WIDTH), f32),
            dma((10, 2, 4)), dma((10, 2)),
            dma((2, 3)), dma((2, 3)), dma((2, 2)), dma((2, 2)), dma((2, 3)), dma((2, 3)),
            dma((n_ctx,)), dma((n_ctx,)), dma((n_dp,)), dma((n_dp,)),
        ],
        compiler_params=pltpu.CompilerParams(
            collective_id=0, has_side_effects=True, vmem_limit_bytes=60 * 2**20
        ),
        name="fused_mixer_attention",
    )(q, k, v, seg, x, b, c, step, rate, skip, g)


def hand_over_kernel(a_in, m_in, g_in, a_out, m_out, g_out, held, in_sem, out_sem):
    rows = a_in.shape[0] // PIECES
    pieces = [(j, i, pl.ds(i * rows, rows)) for i in range(PIECES) for j in range(2)]
    come = [
        pltpu.make_async_copy((a_in, m_in)[j].at[at], held.at[j, at], in_sem.at[j, i])
        for j, i, at in pieces
    ]
    leave = [
        pltpu.make_async_copy(held.at[j, at], (a_out, m_out)[j].at[at], out_sem.at[j, i])
        for j, i, at in pieces
    ]
    for copy in come:
        copy.start()
    g_out[...] = g_in[0, :SSD_HEADS]
    for copy, following in zip(come, leave):
        copy.wait()
        following.start()
    for copy in leave:
        copy.wait()


def hand_over(a, m, g):
    hbm, vmem = pl.BlockSpec(memory_space=pl.ANY), pl.BlockSpec(memory_space=pltpu.VMEM)
    return pl.pallas_call(
        hand_over_kernel,
        out_shape=(
            jax.ShapeDtypeStruct(a.shape, a.dtype),
            jax.ShapeDtypeStruct(m.shape, m.dtype),
            jax.ShapeDtypeStruct((SSD_HEADS,), f32),
        ),
        in_specs=[hbm, hbm, vmem],
        out_specs=(hbm, hbm, vmem),
        scratch_shapes=[
            pltpu.VMEM((2, *a.shape), a.dtype),
            pltpu.SemaphoreType.DMA((2, PIECES)),
            pltpu.SemaphoreType.DMA((2, PIECES)),
        ],
        name="hand_over",
    )(a, m, g)


def on_device(
    queries, keys, values, segment_ids, ssd_input, b_matrix, c_matrix, step_size,
    decay_log, skip_gain, cotangent,
):
    attention, mixed, decay_grad = fused(
        queries[0], keys[0], values[0], segment_ids, ssd_input[0], b_matrix[0], c_matrix[0],
        step_size[0], decay_log, skip_gain, cotangent[0],
    )
    attention, mixed, decay_grad = hand_over(attention, mixed, decay_grad)
    return attention[None], mixed[None], decay_grad


def solution(mesh):
    tok = P("dp", "ctx", None)
    return jax.shard_map(
        on_device,
        mesh=mesh,
        in_specs=(tok, tok, tok, P("dp", "ctx"), tok, tok, tok, P("dp", None, "ctx"), P(), P(), tok),
        out_specs=(tok, tok, P()),
        check_vma=False,
    )
```
